1024 devices in a mesh: gx: 32 (over y_lo, x, core), gy: 4 (over y_hi), gz: 8 (over z).
Axes of the slice: x: 8, y: 8 (y_hi: 4, y_lo: 2; y = y_hi * 2 + y_lo), z: 8, core: 2. Of those that a mesh axis runs over, the one named last changes fastest.
Arguments:
- source: float32 [32, 4, 8, 125, 256], P('gx', 'gy', 'gz'), may hold values from -6 to 6
- stiffness: float32 [125, 125], replicated
- relax: float32 [125], replicated, may hold values from 0.1 to 0.2
- owners: int32 [32, 4, 8, 256, 1], P('gx', 'gy', 'gz'), may hold values from 0 to 31; in each aligned block of 256 rows (0 to 255, 256 to 511, ..., all dimensions but the last counted through in order) at most 16 rows name the same one
- material: int32 [32, 4, 8, 256], P('gx', 'gy', 'gz'), may hold values from 0 to 1, as said below
Outputs:
- settled: float32 [32, 4, 8, 125, 512], P('gx', 'gy', 'gz')
- incoming: float32 [32, 4, 8, 6, 25, 256], P('gx', 'gy', 'gz')
The draws below stay inside these ranges and needn't reach their ends.
Inputs may be any that keep to these rules, and one draw needn't show every extreme that they name: `owners`: within one subdomain no owner is named by more than 16 blocks, a bound that some block reaches in every draw. `material`: in each vertical column of blocks, the blocks below a seafloor depth drawn per column are elastic and those above are acoustic.
All inputs are finite; a program needn't handle non-finite values.
Results may differ from the reference program's by a relative error of at most 0.0001.
Values sent between devices are 32-bit elements; how exact they have to be, the bound alone decides.
A program may use at most 32 MiB of HBM per device.

```python
import math
import jax
import jax.numpy as jnp
import numpy as np
from jax import lax

NODES = 125
FACE = 25
SWEEPS_E = 8
SWEEPS_A = 2
ITERS = 2
BX = 4
BY = 8
BZ = 8
E_DEV = 256
CAP = 16
N_GX = 32
N_GY = 4
N_GZ = 8


def draw_stiffness(key, part):
    key = jax.random.fold_in(key, 11)
    first, second = jax.random.split(key, 2)
    diag_vals = jax.random.uniform(first, (NODES,), jnp.float32, 2.5, 4.0)
    offdiag = jax.random.uniform(second, (NODES, NODES), jnp.float32, -1.0, 1.0)
    offdiag = offdiag * (1.2 / (NODES - 1))
    unit = jnp.eye(NODES, dtype=jnp.float32)
    return offdiag * (1.0 - unit) + unit * diag_vals[None, :]


def draw_material(key, part):
    key = jax.random.fold_in(key, 23)
    depth_total = BZ * N_GZ
    floor_depth = jax.random.randint(key, (N_GX, N_GY, BX * BY), depth_total // 4, 3 * depth_total // 4 + 1)
    blocks = jnp.arange(BX * BY * BZ, dtype=jnp.int32)
    column = blocks // BZ
    depth = jnp.arange(N_GZ, dtype=jnp.int32)[:, None] * BZ + (blocks % BZ)[None, :]
    floor_full = jnp.take(floor_depth, column, axis=2)
    return (depth[None, None, :, :] >= floor_full[:, :, None, :]).astype(jnp.int32)


def level_of(stream_key, shape, shards, low, high):
    def one(axis_at, shards_of):
        heights = jax.random.uniform(jax.random.fold_in(jax.random.fold_in(stream_key, 6), axis_at), (shards_of,), jnp.float32, low / len(shards), high / len(shards))
        return jnp.repeat(jnp.exp(heights), shape[axis_at] // shards_of).reshape((-1,) + (1,) * (len(shape) - axis_at - 1))

    factor_of = one(*shards[0])
    for cut in shards[1:]:
        factor_of = factor_of * one(*cut)
    return factor_of


def shared_out(own_key, own, number, rows, count, top, bound, slope):
    sequence = jax.random.permutation(own_key, count)
    crowded, common = load_shares(count, rows * top, bound, slope, True), load_shares(count, rows * top, bound, slope, False)
    places = jnp.arange(count)

    def named(lengths, offset_by):
        used = int((lengths > 0).sum())
        fixed = max(1, used // 4)
        shifted = fixed + (places - fixed + offset_by * (used - fixed)) % max(1, count - fixed)
        return jnp.zeros((count,), jnp.int32).at[sequence[jnp.where(places < fixed, places, shifted)]].set(jnp.asarray(lengths, jnp.int32))

    lengths = jnp.where(number % 4 == 0, named(crowded, number // 4), named(common, number - number // 4 - 1))
    mixed = jax.random.permutation(jax.random.fold_in(own, 3), count)
    donor, taker = mixed[0:count // 2 * 2:2], mixed[1:count // 2 * 2:2]
    margin = jnp.minimum(lengths[donor] - 1, bound - lengths[taker]) // 2
    margin = jnp.where((donor == sequence[0]) | (taker == sequence[0]) | (lengths[taker] == 0), 0, jnp.maximum(margin, 0))
    shifted = jax.random.randint(jax.random.fold_in(own, 4), (count // 2,), 0, 1 << 20) % (margin + 1)
    lengths = lengths.at[donor].add(-shifted).at[taker].add(shifted)
    items = jnp.searchsorted(jnp.cumsum(lengths), jnp.arange(rows * top), side="right").astype(jnp.int32)
    listing = items.reshape(top, rows).T
    listing = listing[jax.random.permutation(jax.random.fold_in(own, 1), rows)]
    offset_by = jax.random.randint(jax.random.fold_in(own, 2), (rows, 1), 0, top)
    return jnp.take_along_axis(listing, (jnp.arange(top)[None, :] + offset_by) % top, axis=1)


def load_shares(number_of, total, reach, skew, full):
    weights = [(1 << 20) // math.isqrt(grade ** skew) + 1 for grade in range(1, number_of + 1)]
    largest = reach if full else min(reach, max(-(-total // number_of), total * weights[0] // sum(weights)))
    least = 1 if total - largest >= number_of - 1 else 0
    counts, surplus = [largest] + [least] * (number_of - 1), total - largest - least * (number_of - 1)
    while surplus > 0:
        movable = [i for i in range(1, number_of) if counts[i] < largest] or [i for i in range(1, number_of) if counts[i] < reach]
        mass, budget = sum([weights[i] for i in movable]), surplus
        for i in movable:
            more = min(reach - counts[i], max(1, budget * weights[i] // mass), surplus)
            counts[i] = counts[i] + more
            surplus = surplus - more
    return np.array(counts)


def bell_draw(own_key, shape, scale, most, pieces=(), kind=jnp.bfloat16):
    gain = level_of(own_key, shape, pieces, -0.22, 0.18) if pieces else 1.0
    values = jax.random.normal(own_key, shape, jnp.float32) * scale * gain
    return jnp.minimum(jnp.maximum(values, -most), most).astype(kind)


def setup_inputs(seed: int = 0) -> dict:
    keys = jax.random.split(jax.random.key(seed), 6)
    source = bell_draw(keys[0], (N_GX, N_GY, N_GZ, NODES, E_DEV), 1.0, 6.0, ((0, 32), (1, 4), (2, 8)), jnp.float32)
    stiffness = draw_stiffness(jax.random.fold_in(keys[5], 71), 0)
    relax = jnp.clip(jnp.exp(jax.random.uniform(keys[2], (NODES,), jnp.float32, math.log(0.1), math.log(0.2))), 0.1, 0.2)
    owners_keys = jax.random.split(jax.random.fold_in(keys[3], 1), N_GX * N_GY * N_GZ * E_DEV // E_DEV)
    owners_turns = jax.random.permutation(jax.random.fold_in(keys[3], 3), N_GX * N_GY * N_GZ * E_DEV // E_DEV)
    owners = jax.vmap(lambda own, number: shared_out(jax.random.fold_in(keys[3], 2), own, number, E_DEV, N_GX, 1, CAP, 2))(owners_keys, owners_turns).reshape((N_GX, N_GY, N_GZ, E_DEV, 1))
    material = draw_material(jax.random.fold_in(keys[5], 71), 0)
    return dict(source=source, stiffness=stiffness, relax=relax, owners=owners, material=material)


robin_gain = 1.0


def face_table():
    grid = np.arange(125).reshape(5, 5, 5)
    return np.stack([grid[0].ravel(), grid[4].ravel(), grid[:, 0].ravel(), grid[:, 4].ravel(), grid[:, :, 0].ravel(), grid[:, :, 4].ravel()])


def add_traces(field, traces, table):
    result = field
    for side in range(6):
        result = result.at[..., table[side], :].add(traces[..., side, :, :])
    return result


def relaxation(rhs, matf, stiffness, relax):
    scale = 1.0 + 2.0 * matf
    field = jnp.zeros_like(rhs)
    for sweep in range(SWEEPS_E):
        applied = jnp.einsum("nm,...me->...ne", stiffness, field, precision=lax.Precision.HIGHEST)
        active = 1.0 if sweep < SWEEPS_A else matf
        field = field + active * (relax[:, None] * ((rhs - scale * applied) / scale))
    return field


def to_global(values):
    chans = values.shape[3]
    shaped = values.reshape(N_GX, N_GY, N_GZ, chans, BX, BY, BZ)
    shaped = jnp.transpose(shaped, (3, 0, 4, 1, 5, 2, 6))
    return shaped.reshape(chans, N_GX * BX, N_GY * BY, N_GZ * BZ)


def from_global(values):
    chans = values.shape[0]
    shaped = values.reshape(chans, N_GX, BX, N_GY, BY, N_GZ, BZ)
    shaped = jnp.transpose(shaped, (1, 3, 5, 0, 2, 4, 6))
    return shaped.reshape(N_GX, N_GY, N_GZ, chans, BX * BY * BZ)


def pass_traces(outgoing):
    flat = to_global(outgoing.reshape(N_GX, N_GY, N_GZ, 6 * FACE, BX * BY * BZ))
    flat = flat.reshape(6, FACE, N_GX * BX, N_GY * BY, N_GZ * BZ)
    lower_x = jnp.pad(flat[1], ((0, 0), (1, 0), (0, 0), (0, 0)))[:, :-1]
    upper_x = jnp.pad(flat[0], ((0, 0), (0, 1), (0, 0), (0, 0)))[:, 1:]
    lower_y = jnp.pad(flat[3], ((0, 0), (0, 0), (1, 0), (0, 0)))[:, :, :-1]
    upper_y = jnp.pad(flat[2], ((0, 0), (0, 0), (0, 1), (0, 0)))[:, :, 1:]
    lower_z = jnp.pad(flat[5], ((0, 0), (0, 0), (0, 0), (1, 0)))[:, :, :, :-1]
    upper_z = jnp.pad(flat[4], ((0, 0), (0, 0), (0, 0), (0, 1)))[:, :, :, 1:]
    stacked = jnp.stack([lower_x, upper_x, lower_y, upper_y, lower_z, upper_z])
    back = from_global(stacked.reshape(6 * FACE, N_GX * BX, N_GY * BY, N_GZ * BZ))
    return back.reshape(N_GX, N_GY, N_GZ, 6, FACE, BX * BY * BZ)


def reference(source, stiffness, relax, owners, material):
    table = face_table()
    matf = material.astype(jnp.float32)[:, :, :, None, :]
    incoming = jnp.zeros((N_GX, N_GY, N_GZ, 6, FACE, BX * BY * BZ), jnp.float32)
    field = source
    for step in range(ITERS):
        rhs = add_traces(source, incoming, table)
        field = relaxation(rhs, matf, stiffness, relax)
        outgoing = -incoming + 2.0 * robin_gain * field[:, :, :, table, :]
        incoming = pass_traces(outgoing)
    owner = owners[..., 0]
    onehot = (owner[..., None] == jnp.arange(N_GX, dtype=jnp.int32)).astype(jnp.int32)
    rank = jnp.sum(jnp.cumsum(onehot, axis=3) * onehot, axis=-1) - 1
    src = jnp.arange(N_GX, dtype=jnp.int32)[:, None, None, None]
    ycol = jnp.arange(N_GY, dtype=jnp.int32)[None, :, None, None]
    zcol = jnp.arange(N_GZ, dtype=jnp.int32)[None, None, :, None]
    slot = (src * CAP + rank).astype(jnp.int32)
    ones = jnp.zeros_like(owner)
    settled = jnp.zeros((N_GX, N_GY, N_GZ, NODES, N_GX * CAP), jnp.float32)
    settled = settled.at[owner, ycol + ones, zcol + ones, :, slot].set(jnp.swapaxes(field, -1, -2))
    return settled, incoming
```

```python
import functools

import jax
import jax.numpy as jnp
from jax import lax
from jax.experimental import pallas as pl
from jax.experimental.pallas import tpu as pltpu
from jax.sharding import PartitionSpec as P

NODES = 125
FACE = 25
LANES = 128
COUNT = 256
SLOTS = 512
CAP = 16
GROUPS = 32
FACE_ROWS = 32
STACK = 6 * FACE_ROWS
MESH = pl.DeviceIdType.MESH
F32 = jnp.float32
BF16 = jnp.bfloat16
HIGHEST = lax.Precision.HIGHEST

HALO = ((0, 16), (16, 16), (32, 8), (40, 8), (48, 8), (56, 8))
HALO_ROWS = 64
ORDER = tuple(
    dy * 16 + dx * 2 + dc
    for dx in (4, 3, 5, 2, 6, 1, 7, 0)
    for dy in (1, 0)
    for dc in (1, 0)
    if dy + dx + dc
)


def iota(shape, dim):
    return lax.broadcasted_iota(jnp.int32, shape, dim)


def matmul(left, right):
    return lax.dot_general(
        left, right, (((1,), (0,)), ((), ())), preferred_element_type=F32
    )


def matmul_t(left, right):
    return lax.dot_general(
        left, right, (((1,), (1,)), ((), ())), preferred_element_type=F32
    )


def full(left, right):
    return lax.dot_general(
        left, right, (((1,), (0,)), ((), ())), precision=HIGHEST, preferred_element_type=F32
    )


def halves(values):
    high = values.astype(BF16)
    return high, (values - high.astype(F32)).astype(BF16)


def roll(values, shift):
    shift = shift % LANES
    return pltpu.roll(values, shift, 1) if shift else values


def face_rows():
    m = iota((FACE_ROWS, LANES), 0)
    node = iota((FACE_ROWS, LANES), 1)
    a = sum((m >= cut).astype(jnp.int32) for cut in (5, 10, 15, 20))
    b = m - 5 * a
    picks = (m, m + 100, 25 * a + b, 25 * a + b + 20, 5 * m, 5 * m + 4)
    faces = [jnp.where((node == pick) & (m < FACE), 1.0, 0.0) for pick in picks]
    return jnp.concatenate(faces, axis=0).astype(BF16)


def pieces(face):
    return [(r, t, face[8 * r : 8 * r + 8, LANES * t : LANES * t + LANES]) for r in range(4) for t in range(2)]


def total(terms):
    while len(terms) > 1:
        terms = [sum(terms[i : i + 2]) for i in range(0, len(terms), 2)]
    return terms[0]


def pack_halo(out, tx):
    lane = iota((8, LANES), 1)
    z, y = lane & 7, (lane >> 3) & 7
    low = lane < 64
    face = lambda f: out[FACE_ROWS * f : FACE_ROWS * (f + 1)]
    piece = {f: {(r, t): v for r, t, v in pieces(face(f))} for f in range(6)}
    for j in range(2):
        tx[8 * j : 8 * j + 8] = jnp.where(low, roll(piece[1][2 * j, 1], 64), piece[1][2 * j + 1, 1])
        tx[16 + 8 * j : 24 + 8 * j] = jnp.where(low, piece[0][2 * j, 0], roll(piece[0][2 * j + 1, 0], 64))

    def gather(f, keep, shift):
        return total([
            roll(jnp.where(keep, piece[f][r, t], 0.0), shift(2 * r + t)) for r in range(4) for t in range(2)
        ])

    tx[32:40] = gather(3, y == 7, lambda q: 8 * q - 56)
    tx[40:48] = gather(2, y == 0, lambda q: 8 * q)
    tx[48:56] = gather(5, z == 7, lambda q: q - 7)
    tx[56:64] = gather(4, z == 0, lambda q: q)


def shift_inside(out, inc):
    lane = iota((FACE_ROWS, LANES), 1)
    z, y = lane & 7, (lane >> 3) & 7
    low = lane < 64
    tile = lambda f, t: out[FACE_ROWS * f : FACE_ROWS * (f + 1), LANES * t : LANES * (t + 1)]

    def put(f, t, values):
        inc[t, FACE_ROWS * f : FACE_ROWS * (f + 1)] = values

    a, b = roll(tile(1, 0), 64), roll(tile(1, 1), 64)
    put(0, 0, jnp.where(low, 0.0, a))
    put(0, 1, jnp.where(low, a, b))
    a, b = roll(tile(0, 0), 64), roll(tile(0, 1), 64)
    put(1, 0, jnp.where(low, a, b))
    put(1, 1, jnp.where(low, b, 0.0))
    for t in range(2):
        put(2, t, jnp.where(y == 0, 0.0, roll(tile(3, t), 8)))
        put(3, t, jnp.where(y == 7, 0.0, roll(tile(2, t), -8)))
        put(4, t, jnp.where(z == 0, 0.0, roll(tile(5, t), 1)))
        put(5, t, jnp.where(z == 7, 0.0, roll(tile(4, t), -1)))


def add_halo(rx, inc, inner):
    lane = iota((8, LANES), 1)
    z, y = lane & 7, (lane >> 3) & 7
    low = lane < 64
    has = [jnp.full((8, LANES), flag, jnp.int32) > 0 for flag in inner]

    def add(f, r, t, keep, values):
        rows = slice(FACE_ROWS * f + 8 * r, FACE_ROWS * f + 8 * r + 8)
        inc[t, rows] = jnp.where(keep, values, inc[t, rows])

    for j in range(2):
        part = rx[8 * j : 8 * j + 8]
        add(0, 2 * j, 0, low & has[0], part)
        add(0, 2 * j + 1, 0, low & has[0], roll(part, 64))
        part = rx[16 + 8 * j : 24 + 8 * j]
        add(1, 2 * j, 1, (lane >= 64) & has[1], roll(part, 64))
        add(1, 2 * j + 1, 1, (lane >= 64) & has[1], part)
    for r in range(4):
        for t in range(2):
            q = 2 * r + t
            add(2, r, t, (y == 0) & has[2], roll(rx[32:40], -8 * q))
            add(3, r, t, (y == 7) & has[3], roll(rx[40:48], 56 - 8 * q))
            add(4, r, t, (z == 0) & has[4], roll(rx[48:56], -q))
            add(5, r, t, (z == 7) & has[5], roll(rx[56:64], 7 - q))


def kernel(
    source_hbm, stiffness_hbm, relax_hbm, owners_hbm, material_hbm,
    settled_hbm, incoming_hbm,
    src, stiff, relax, owner, mat, kpad, rpad, packer, moved, landed, turned, tx, rx, inc,
    in_sem, out_sem, halo_send, halo_recv, move_send, move_recv,
):
    gx, gy, gz = (lax.axis_index(axis) for axis in ("gx", "gy", "gz"))
    loads = [
        pltpu.make_async_copy(stiffness_hbm, stiff, in_sem.at[0]),
        pltpu.make_async_copy(relax_hbm, relax, in_sem.at[1]),
        pltpu.make_async_copy(source_hbm.at[:, 0, pl.ds(0, LANES)], src.at[0, pl.ds(0, NODES)], in_sem.at[2]),
        pltpu.make_async_copy(source_hbm.at[:, 0, pl.ds(LANES, LANES)], src.at[1, pl.ds(0, NODES)], in_sem.at[5]),
        pltpu.make_async_copy(owners_hbm, owner, in_sem.at[3]),
        pltpu.make_async_copy(material_hbm, mat, in_sem.at[4]),
    ]
    for t in range(2):
        src[t, 120:128] = jnp.zeros((8, LANES), F32)
    for load in loads:
        load.start()

    my_y, my_x, my_c = gx // 16, (gx // 2) % 8, gx % 2

    def peer(chunk):
        dy, dx, dc = chunk // 16, (chunk // 2) % 8, chunk % 2
        return ((my_y + dy) % 2) * 16 + ((my_x + dx) % 8) * 2 + (my_c + dc) % 2

    barrier = pltpu.get_barrier_semaphore()
    for chunk in ORDER:
        pl.semaphore_signal(barrier, 1, device_id=(peer(chunk), gy, gz), device_id_type=MESH)
    sides = (
        ((gx + 1) % 32, gy, gz), ((gx + 31) % 32, gy, gz),
        (gx, (gy + 1) % 4, gz), (gx, (gy + 3) % 4, gz),
        (gx, gy, (gz + 1) % 8), (gx, gy, (gz + 7) % 8),
    )
    for side in sides[2:]:
        pl.semaphore_signal(barrier, 1, device_id=side, device_id_type=MESH)
    inner = (gx, 31 - gx, gy, 3 - gy, gz, 7 - gz)

    kpad[...] = jnp.zeros((LANES, LANES), F32)
    rpad[...] = jnp.zeros((8, LANES), F32)
    loads[0].wait()
    loads[1].wait()
    kpad[0:NODES, 0:NODES] = stiff[...]
    rpad[0:1, 0:NODES] = relax[...]
    eye = iota((LANES, LANES), 0) == iota((LANES, LANES), 1)
    row = jnp.broadcast_to(rpad[0:1], (LANES, LANES))
    diag = jnp.where(eye, row, 0.0)
    col = jnp.sum(diag, axis=1, keepdims=True)
    scaled = col * kpad[...]
    step = jnp.where(eye, 1.0, 0.0) - scaled
    sum2 = 2.0 * diag - scaled * row
    step2 = full(step, step)
    sum4 = sum2 + full(step2, sum2)
    step4 = full(step2, step2)
    sum8 = sum4 + full(step4, sum4)
    elastic_op, acoustic_op = sum8 * (1.0 / 3.0), sum2

    for load in loads[2:]:
        load.wait()
    elastic = jnp.broadcast_to(mat[...], (LANES, COUNT)) > 0
    source = jnp.concatenate([src[0], src[1]], axis=1)
    field = jnp.where(elastic, full(elastic_op, source), full(acoustic_op, source))
    pick = face_rows()
    high, low = halves(field)
    faces = matmul(pick, high) + matmul(pick, low)
    out = 2.0 * faces
    pack_halo(out, tx.at[0])

    def halo_copies(step):
        return [
            pltpu.make_async_remote_copy(
                src_ref=tx.at[step, pl.ds(at, rows)],
                dst_ref=rx.at[step, pl.ds(at, rows)],
                send_sem=halo_send.at[step, i],
                recv_sem=halo_recv.at[step, i],
                device_id=sides[i],
                device_id_type=MESH,
            )
            for i, (at, rows) in enumerate(HALO)
        ]

    pl.semaphore_wait(barrier, len(ORDER) + 4)
    first = halo_copies(0)
    for copy in first:
        copy.start()

    shift_inside(out, inc)
    ops = []
    for op in (elastic_op, acoustic_op):
        high, low = halves(op)
        nodes = matmul_t(high, pick) + matmul_t(low, pick)
        high, low = halves(nodes)
        ops.append((high, low))
    on_nodes = [jnp.concatenate([ops[0][i], ops[1][i]], axis=0) for i in range(2)]
    on_faces = [
        jnp.concatenate([matmul(pick, ops[0][i]), matmul(pick, ops[1][i])], axis=0).astype(BF16) for i in range(2)
    ]

    names = owner[...]
    named = iota((GROUPS, COUNT), 0) == jnp.broadcast_to(names, (GROUPS, COUNT))
    before = jnp.where(iota((COUNT, COUNT), 0) < iota((COUNT, COUNT), 1), 1.0, 0.0).astype(BF16)
    counts = matmul(jnp.where(named, 1.0, 0.0).astype(BF16), before)
    rank = jnp.sum(jnp.where(named, counts, 0.0), axis=0, keepdims=True).astype(jnp.int32)
    chunk = (
        (((names >> 4) ^ my_y) << 4)
        | ((((names >> 1) - my_x) & 7) << 1)
        | ((names & 1) ^ my_c)
    )
    slot = chunk * CAP + rank
    for k in range(4):
        here = iota((LANES, COUNT), 0) + k * LANES == jnp.broadcast_to(slot, (LANES, COUNT))
        packer[k * LANES : (k + 1) * LANES] = jnp.where(here, 1.0, 0.0).astype(BF16)

    for copy in first:
        copy.wait_recv()
    add_halo(rx.at[0], inc, inner)

    incoming = jnp.concatenate([inc[0], inc[1]], axis=1)
    high, low = halves(incoming)

    def on_traces(op):
        return matmul(op[0], high) + matmul(op[0], low) + matmul(op[1], high)

    change = on_traces(on_nodes)
    field = field + jnp.where(elastic, change[0:LANES], change[LANES : 2 * LANES])
    both = jnp.concatenate(halves(field), axis=0)
    for k in range(4):
        part = matmul_t(packer[k * LANES : (k + 1) * LANES], both)
        moved[k * LANES : (k + 1) * LANES] = part[:, 0:LANES] + part[:, LANES : 2 * LANES]
    moves = []
    for chunk in ORDER:
        copy = pltpu.make_async_remote_copy(
            src_ref=moved.at[pl.ds(chunk * CAP, CAP)],
            dst_ref=landed.at[pl.ds(pl.multiple_of(gx * CAP, CAP), CAP)],
            send_sem=move_send.at[chunk],
            recv_sem=move_recv.at[chunk],
            device_id=(peer(chunk), gy, gz),
            device_id_type=MESH,
        )
        copy.start()
        moves.append(copy)
    landed[pl.ds(pl.multiple_of(gx * CAP, CAP), CAP)] = moved[0:CAP]

    change = on_traces(on_faces)
    face_elastic = jnp.broadcast_to(mat[...], (STACK, COUNT)) > 0
    faces = faces + jnp.where(face_elastic, change[0:STACK], change[STACK : 2 * STACK])
    out = 2.0 * faces - incoming
    pack_halo(out, tx.at[1])
    second = halo_copies(1)
    for copy in second:
        copy.start()
    shift_inside(out, inc)
    for copy in second:
        copy.wait_recv()
    add_halo(rx.at[1], inc, inner)
    results = []
    for f in range(6):
        for t in range(2):
            results.append(
                pltpu.make_async_copy(
                    inc.at[t, pl.ds(f * FACE_ROWS, FACE)],
                    incoming_hbm.at[f, :, 0, pl.ds(t * LANES, LANES)],
                    out_sem.at[2 * f + t],
                )
            )
            results[-1].start()

    for copy in moves:
        copy.wait_recv()
    for k in range(4):
        turned[k] = landed[k * LANES : (k + 1) * LANES].T
        results.append(
            pltpu.make_async_copy(
                turned.at[k, pl.ds(0, NODES)], settled_hbm.at[:, 0, pl.ds(k * LANES, LANES)], out_sem.at[12 + k]
            )
        )
        results[-1].start()
    for copy in first + second + moves:
        copy.wait_send()
    for copy in results:
        copy.wait()


def shards(source, stiffness, relax, owners, material):
    anywhere = pl.BlockSpec(memory_space=pl.ANY)
    settled, incoming = pl.pallas_call(
        kernel,
        out_shape=(
            jax.ShapeDtypeStruct((NODES, 1, SLOTS), F32),
            jax.ShapeDtypeStruct((6, FACE, 1, COUNT), F32),
        ),
        in_specs=[anywhere] * 5,
        out_specs=(anywhere, anywhere),
        scratch_shapes=[
            pltpu.VMEM((2, LANES, LANES), F32),
            pltpu.VMEM((NODES, NODES), F32),
            pltpu.VMEM((1, NODES), F32),
            pltpu.VMEM((1, COUNT), jnp.int32),
            pltpu.VMEM((1, COUNT), jnp.int32),
            pltpu.VMEM((LANES, LANES), F32),
            pltpu.VMEM((8, LANES), F32),
            pltpu.VMEM((SLOTS, COUNT), BF16),
            pltpu.VMEM((SLOTS, LANES), F32),
            pltpu.VMEM((SLOTS, LANES), F32),
            pltpu.VMEM((4, LANES, LANES), F32),
            pltpu.VMEM((2, HALO_ROWS, LANES), F32),
            pltpu.VMEM((2, HALO_ROWS, LANES), F32),
            pltpu.VMEM((2, STACK, LANES), F32),
            pltpu.SemaphoreType.DMA((6,)),
            pltpu.SemaphoreType.DMA((16,)),
            pltpu.SemaphoreType.DMA((2, 6)),
            pltpu.SemaphoreType.DMA((2, 6)),
            pltpu.SemaphoreType.DMA((GROUPS,)),
            pltpu.SemaphoreType.DMA((GROUPS,)),
        ],
        compiler_params=pltpu.CompilerParams(
            collective_id=0, has_side_effects=True, vmem_limit_bytes=48 * 1024 * 1024
        ),
    )(
        source.reshape(NODES, 1, COUNT),
        stiffness,
        relax.reshape(1, NODES),
        owners.reshape(1, COUNT),
        material.reshape(1, COUNT),
    )
    return (
        settled.reshape(1, 1, 1, NODES, SLOTS),
        incoming.reshape(1, 1, 1, 6, FACE, COUNT),
    )


def solution(mesh):
    return jax.shard_map(
        shards,
        mesh=mesh,
        in_specs=(
            P("gx", "gy", "gz", None, None),
            P(),
            P(),
            P("gx", "gy", "gz", None, None),
            P("gx", "gy", "gz", None),
        ),
        out_specs=(P("gx", "gy", "gz", None, None), P("gx", "gy", "gz", None, None, None)),
        check_vma=False,
    )
```

```python
import functools

import jax
import jax.numpy as jnp
from jax import lax
from jax.experimental import pallas as pl
from jax.experimental.pallas import tpu as pltpu
from jax.sharding import PartitionSpec as P

NODES = 125
FACE = 25
LANES = 128
COUNT = 256
SLOTS = 512
CAP = 16
GROUPS = 32
FACE_ROWS = 32
STACK = 6 * FACE_ROWS
MESH = pl.DeviceIdType.MESH
F32 = jnp.float32
BF16 = jnp.bfloat16
HIGHEST = lax.Precision.HIGHEST

HALO = ((0, 16), (16, 16), (32, 8), (40, 8), (48, 8), (56, 8))
HALO_ROWS = 64
ORDER = tuple(
    dy * 16 + dx * 2 + dc
    for dx in (0, 1, 7, 2, 6, 3, 5, 4)
    for dy in (0, 1)
    for dc in (1, 0)
    if dy + dx + dc
)


def iota(shape, dim):
    return lax.broadcasted_iota(jnp.int32, shape, dim)


def matmul(left, right):
    return lax.dot_general(
        left, right, (((1,), (0,)), ((), ())), preferred_element_type=F32
    )


def matmul_t(left, right):
    return lax.dot_general(
        left, right, (((1,), (1,)), ((), ())), preferred_element_type=F32
    )


def full(left, right):
    return lax.dot_general(
        left, right, (((1,), (0,)), ((), ())), precision=HIGHEST, preferred_element_type=F32
    )


def halves(values):
    high = values.astype(BF16)
    return high, (values - high.astype(F32)).astype(BF16)


def roll(values, shift):
    shift = shift % LANES
    return pltpu.roll(values, shift, 1) if shift else values


def face_rows():
    m = iota((FACE_ROWS, LANES), 0)
    node = iota((FACE_ROWS, LANES), 1)
    a = sum((m >= cut).astype(jnp.int32) for cut in (5, 10, 15, 20))
    b = m - 5 * a
    picks = (m, m + 100, 25 * a + b, 25 * a + b + 20, 5 * m, 5 * m + 4)
    faces = [jnp.where((node == pick) & (m < FACE), 1.0, 0.0) for pick in picks]
    return jnp.concatenate(faces, axis=0).astype(BF16)


def pieces(face):
    return [(r, t, face[8 * r : 8 * r + 8, LANES * t : LANES * t + LANES]) for r in range(4) for t in range(2)]


def total(terms):
    while len(terms) > 1:
        terms = [sum(terms[i : i + 2]) for i in range(0, len(terms), 2)]
    return terms[0]


def pack_halo(out, tx):
    lane = iota((8, LANES), 1)
    z, y = lane & 7, (lane >> 3) & 7
    low = lane < 64
    face = lambda f: out[FACE_ROWS * f : FACE_ROWS * (f + 1)]
    piece = {f: {(r, t): v for r, t, v in pieces(face(f))} for f in range(6)}
    for j in range(2):
        tx[8 * j : 8 * j + 8] = jnp.where(low, roll(piece[1][2 * j, 1], 64), piece[1][2 * j + 1, 1])
        tx[16 + 8 * j : 24 + 8 * j] = jnp.where(low, piece[0][2 * j, 0], roll(piece[0][2 * j + 1, 0], 64))

    def gather(f, keep, shift):
        return total([
            roll(jnp.where(keep, piece[f][r, t], 0.0), shift(2 * r + t)) for r in range(4) for t in range(2)
        ])

    tx[32:40] = gather(3, y == 7, lambda q: 8 * q - 56)
    tx[40:48] = gather(2, y == 0, lambda q: 8 * q)
    tx[48:56] = gather(5, z == 7, lambda q: q - 7)
    tx[56:64] = gather(4, z == 0, lambda q: q)


def shift_inside(out, inc):
    lane = iota((FACE_ROWS, LANES), 1)
    z, y = lane & 7, (lane >> 3) & 7
    low = lane < 64
    tile = lambda f, t: out[FACE_ROWS * f : FACE_ROWS * (f + 1), LANES * t : LANES * (t + 1)]

    def put(f, t, values):
        inc[t, FACE_ROWS * f : FACE_ROWS * (f + 1)] = values

    a, b = roll(tile(1, 0), 64), roll(tile(1, 1), 64)
    put(0, 0, jnp.where(low, 0.0, a))
    put(0, 1, jnp.where(low, a, b))
    a, b = roll(tile(0, 0), 64), roll(tile(0, 1), 64)
    put(1, 0, jnp.where(low, a, b))
    put(1, 1, jnp.where(low, b, 0.0))
    for t in range(2):
        put(2, t, jnp.where(y == 0, 0.0, roll(tile(3, t), 8)))
        put(3, t, jnp.where(y == 7, 0.0, roll(tile(2, t), -8)))
        put(4, t, jnp.where(z == 0, 0.0, roll(tile(5, t), 1)))
        put(5, t, jnp.where(z == 7, 0.0, roll(tile(4, t), -1)))


def add_halo(rx, inc, inner):
    lane = iota((8, LANES), 1)
    z, y = lane & 7, (lane >> 3) & 7
    low = lane < 64
    has = [jnp.full((8, LANES), inner[i ^ 1].astype(jnp.int32), jnp.int32) > 0 for i in range(6)]

    def add(f, r, t, keep, values):
        rows = slice(FACE_ROWS * f + 8 * r, FACE_ROWS * f + 8 * r + 8)
        inc[t, rows] = jnp.where(keep, values, inc[t, rows])

    for j in range(2):
        part = rx[8 * j : 8 * j + 8]
        add(0, 2 * j, 0, low & has[0], part)
        add(0, 2 * j + 1, 0, low & has[0], roll(part, 64))
        part = rx[16 + 8 * j : 24 + 8 * j]
        add(1, 2 * j, 1, (lane >= 64) & has[1], roll(part, 64))
        add(1, 2 * j + 1, 1, (lane >= 64) & has[1], part)
    for r in range(4):
        for t in range(2):
            q = 2 * r + t
            add(2, r, t, (y == 0) & has[2], roll(rx[32:40], -8 * q))
            add(3, r, t, (y == 7) & has[3], roll(rx[40:48], 56 - 8 * q))
            add(4, r, t, (z == 0) & has[4], roll(rx[48:56], -q))
            add(5, r, t, (z == 7) & has[5], roll(rx[56:64], 7 - q))


def kernel(
    source_hbm, stiffness_hbm, relax_hbm, owners_hbm, material_hbm,
    landed, inc,
    src, stiff, relax, owner, mat, kpad, rpad, packer, moved, tx, rx,
    in_sem, halo_send, halo_recv, move_send, move_recv,
):
    gx, gy, gz = (lax.axis_index(axis) for axis in ("gx", "gy", "gz"))
    loads = [
        pltpu.make_async_copy(stiffness_hbm, stiff, in_sem.at[0]),
        pltpu.make_async_copy(relax_hbm, relax, in_sem.at[1]),
        pltpu.make_async_copy(source_hbm.at[:, 0, pl.ds(0, LANES)], src.at[0, pl.ds(0, NODES)], in_sem.at[2]),
        pltpu.make_async_copy(source_hbm.at[:, 0, pl.ds(LANES, LANES)], src.at[1, pl.ds(0, NODES)], in_sem.at[5]),
        pltpu.make_async_copy(owners_hbm, owner, in_sem.at[3]),
        pltpu.make_async_copy(material_hbm, mat, in_sem.at[4]),
    ]
    for t in range(2):
        src[t, 120:128] = jnp.zeros((8, LANES), F32)
    for load in loads:
        load.start()
    rx[...] = jnp.zeros_like(rx)

    my_y, my_x, my_c = gx // 16, (gx // 2) % 8, gx % 2

    def peer(chunk):
        dy, dx, dc = chunk // 16, (chunk // 2) % 8, chunk % 2
        return ((my_y + dy) % 2) * 16 + ((my_x + dx) % 8) * 2 + (my_c + dc) % 2

    sides = (
        (gx + 1, gy, gz), (gx - 1, gy, gz), (gx, gy + 1, gz), (gx, gy - 1, gz), (gx, gy, gz + 1), (gx, gy, gz - 1),
    )
    there = (gx < 31, gx > 0, gy < 3, gy > 0, gz < 7, gz > 0)
    around = sum(flag.astype(jnp.int32) for flag in there[2:])
    barrier = pltpu.get_barrier_semaphore()

    def greet(device):
        pl.semaphore_signal(barrier, 1, device_id=device, device_id_type=MESH)

    for i in range(2, 6):
        pl.when(there[i])(functools.partial(greet, sides[i]))

    @pl.when(gx == 0)
    def _():
        pl.semaphore_wait(barrier, GROUPS - 1 + around)
        for chunk in ORDER:
            greet((peer(chunk), gy, gz))

    @pl.when(gx > 0)
    def _():
        for chunk in ORDER:
            other = peer(chunk)
            pl.when(other > 0)(functools.partial(greet, (other, gy, gz)))

    kpad[...] = jnp.zeros((LANES, LANES), F32)
    rpad[...] = jnp.zeros((8, LANES), F32)
    loads[0].wait()
    loads[1].wait()
    kpad[0:NODES, 0:NODES] = stiff[...]
    rpad[0:1, 0:NODES] = relax[...]
    eye = iota((LANES, LANES), 0) == iota((LANES, LANES), 1)
    row = jnp.broadcast_to(rpad[0:1], (LANES, LANES))
    diag = jnp.where(eye, row, 0.0)
    col = jnp.sum(diag, axis=1, keepdims=True)
    scaled = col * kpad[...]
    step = jnp.where(eye, 1.0, 0.0) - scaled
    sum2 = 2.0 * diag - scaled * row
    step2 = full(step, step)
    sum4 = sum2 + full(step2, sum2)
    step4 = full(step2, step2)
    sum8 = sum4 + full(step4, sum4)
    elastic_op, acoustic_op = sum8 * (1.0 / 3.0), sum2

    for load in loads[2:]:
        load.wait()
    elastic = jnp.broadcast_to(mat[...], (LANES, COUNT)) > 0
    source = jnp.concatenate([src[0], src[1]], axis=1)
    field = jnp.where(elastic, full(elastic_op, source), full(acoustic_op, source))
    pick = face_rows()
    high, low = halves(field)
    faces = matmul(pick, high) + matmul(pick, low)
    out = 2.0 * faces
    pack_halo(out, tx.at[0])

    def halo_copy(step, i):
        at, rows = HALO[i]
        return pltpu.make_async_remote_copy(
            src_ref=tx.at[step, pl.ds(at, rows)],
            dst_ref=rx.at[step, pl.ds(at, rows)],
            send_sem=halo_send.at[step, i],
            recv_sem=halo_recv.at[step, i],
            device_id=sides[i],
            device_id_type=MESH,
        )

    def halo_start(step, i, when):
        @pl.when(when)
        def _():
            halo_copy(step, i).start()

    def halo_wait_recv(step):
        for i in range(6):
            @pl.when(there[i ^ 1])
            def _():
                halo_copy(step, i).wait_recv()

    def halo_wait_send(step):
        for i in range(6):
            @pl.when(there[i])
            def _():
                halo_copy(step, i).wait_send()

    @pl.when(gx > 0)
    def _():
        pl.semaphore_wait(barrier, GROUPS - 2 + around)
        greet((0, gy, gz))

    halo_start(0, 0, there[0])
    halo_start(0, 1, gx > 1)
    for i in range(2, 6):
        halo_start(0, i, there[i])

    @pl.when(gx == 1)
    def _():
        pl.semaphore_wait(barrier, 1)
        halo_copy(0, 1).start()

    shift_inside(out, inc)
    ops = []
    for op in (elastic_op, acoustic_op):
        high, low = halves(op)
        nodes = matmul_t(high, pick) + matmul_t(low, pick)
        high, low = halves(nodes)
        ops.append((high, low))
    on_nodes = [jnp.concatenate([ops[0][i], ops[1][i]], axis=0) for i in range(2)]
    on_faces = [
        jnp.concatenate([matmul(pick, ops[0][i]), matmul(pick, ops[1][i])], axis=0).astype(BF16) for i in range(2)
    ]

    names = owner[...]
    named = iota((GROUPS, COUNT), 0) == jnp.broadcast_to(names, (GROUPS, COUNT))
    before = jnp.where(iota((COUNT, COUNT), 0) < iota((COUNT, COUNT), 1), 1.0, 0.0).astype(BF16)
    counts = matmul(jnp.where(named, 1.0, 0.0).astype(BF16), before)
    rank = jnp.sum(jnp.where(named, counts, 0.0), axis=0, keepdims=True).astype(jnp.int32)
    chunk = (
        (((names >> 4) ^ my_y) << 4)
        | ((((names >> 1) - my_x) & 7) << 1)
        | ((names & 1) ^ my_c)
    )
    slot = chunk * CAP + rank
    for k in range(4):
        here = iota((LANES, COUNT), 0) + k * LANES == jnp.broadcast_to(slot, (LANES, COUNT))
        packer[k * LANES : (k + 1) * LANES] = jnp.where(here, 1.0, 0.0).astype(BF16)

    halo_wait_recv(0)
    add_halo(rx.at[0], inc, there)

    incoming = jnp.concatenate([inc[0], inc[1]], axis=1)
    high, low = halves(incoming)

    def on_traces(op):
        return matmul(op[0], high) + matmul(op[0], low) + matmul(op[1], high)

    change = on_traces(on_faces)
    face_elastic = jnp.broadcast_to(mat[...], (STACK, COUNT)) > 0
    faces = faces + jnp.where(face_elastic, change[0:STACK], change[STACK : 2 * STACK])
    out = 2.0 * faces - incoming
    pack_halo(out, tx.at[1])
    change = on_traces(on_nodes)
    field = field + jnp.where(elastic, change[0:LANES], change[LANES : 2 * LANES])
    both = jnp.concatenate(halves(field), axis=0)
    for i in range(6):
        halo_start(1, i, there[i])
    for k in range(4):
        part = matmul_t(packer[k * LANES : (k + 1) * LANES], both)
        moved[k * LANES : (k + 1) * LANES] = part[:, 0:LANES] + part[:, LANES : 2 * LANES]

    mine = pl.ds(pl.multiple_of(gx * CAP, CAP), CAP)

    def move(chunk):
        return pltpu.make_async_remote_copy(
            src_ref=moved.at[pl.ds(pl.multiple_of(chunk * CAP, CAP), CAP)],
            dst_ref=landed.at[mine],
            send_sem=move_send.at[chunk],
            recv_sem=move_recv.at[chunk],
            device_id=(peer(chunk), gy, gz),
            device_id_type=MESH,
        )

    for chunk in ORDER:
        pl.when(peer(chunk) > 0)(lambda chunk=chunk: move(chunk).start())

    @pl.when(gx > 1)
    def _():
        pl.semaphore_wait(barrier, 1)

    @pl.when(gx > 0)
    def _():
        move(my_y * 16 + ((8 - my_x) % 8) * 2 + my_c).start()

    landed[mine] = moved[0:CAP]
    shift_inside(out, inc)
    halo_wait_recv(1)
    add_halo(rx.at[1], inc, there)
    for chunk in ORDER:
        move(chunk).wait_recv()
    halo_wait_send(0)
    halo_wait_send(1)
    for chunk in ORDER:
        move(chunk).wait_send()


def finish(landed, inc, settled_hbm, incoming_hbm, turned, out_sem):
    results = []
    for f in range(6):
        for t in range(2):
            results.append(
                pltpu.make_async_copy(
                    inc.at[t, pl.ds(f * FACE_ROWS, FACE)],
                    incoming_hbm.at[f, :, 0, pl.ds(t * LANES, LANES)],
                    out_sem.at[2 * f + t],
                )
            )
            results[-1].start()
    for k in range(4):
        turned[k] = landed[k * LANES : (k + 1) * LANES].T
        results.append(
            pltpu.make_async_copy(
                turned.at[k, pl.ds(0, NODES)], settled_hbm.at[:, 0, pl.ds(k * LANES, LANES)], out_sem.at[12 + k]
            )
        )
        results[-1].start()
    for copy in results:
        copy.wait()


def shards(source, stiffness, relax, owners, material):
    anywhere = pl.BlockSpec(memory_space=pl.ANY)
    vmem = pl.BlockSpec(memory_space=pltpu.VMEM)
    operands = (
        source.reshape(NODES, 1, COUNT),
        stiffness,
        relax.reshape(1, NODES),
        owners.reshape(1, COUNT),
        material.reshape(1, COUNT),
    )
    landed, inc = pl.pallas_call(
        kernel,
        out_shape=(pltpu.VMEM((SLOTS, LANES), F32), pltpu.VMEM((2, STACK, LANES), F32)),
        in_specs=[anywhere] * 5,
        out_specs=(vmem, vmem),
        scratch_shapes=[
            pltpu.VMEM((2, LANES, LANES), F32),
            pltpu.VMEM((NODES, NODES), F32),
            pltpu.VMEM((1, NODES), F32),
            pltpu.VMEM((1, COUNT), jnp.int32),
            pltpu.VMEM((1, COUNT), jnp.int32),
            pltpu.VMEM((LANES, LANES), F32),
            pltpu.VMEM((8, LANES), F32),
            pltpu.VMEM((SLOTS, COUNT), BF16),
            pltpu.VMEM((SLOTS, LANES), F32),
            pltpu.VMEM((2, HALO_ROWS, LANES), F32),
            pltpu.VMEM((2, HALO_ROWS, LANES), F32),
            pltpu.SemaphoreType.DMA((6,)),
            pltpu.SemaphoreType.DMA((2, 6)),
            pltpu.SemaphoreType.DMA((2, 6)),
            pltpu.SemaphoreType.DMA((GROUPS,)),
            pltpu.SemaphoreType.DMA((GROUPS,)),
        ],
        compiler_params=pltpu.CompilerParams(
            collective_id=0, has_side_effects=True, vmem_limit_bytes=32 * 1024 * 1024
        ),
    )(*(pltpu.with_memory_space_constraint(x, pltpu.HBM) for x in operands))
    settled, incoming = pl.pallas_call(
        finish,
        out_shape=(pltpu.HBM((NODES, 1, SLOTS), F32), pltpu.HBM((6, FACE, 1, COUNT), F32)),
        in_specs=(vmem, vmem),
        out_specs=(anywhere, anywhere),
        scratch_shapes=[pltpu.VMEM((4, LANES, LANES), F32), pltpu.SemaphoreType.DMA((16,))],
        compiler_params=pltpu.CompilerParams(vmem_limit_bytes=32 * 1024 * 1024),
    )(landed, inc)
    return (
        settled.reshape(1, 1, 1, NODES, SLOTS),
        incoming.reshape(1, 1, 1, 6, FACE, COUNT),
    )


def solution(mesh):
    return jax.shard_map(
        shards,
        mesh=mesh,
        in_specs=(
            P("gx", "gy", "gz", None, None),
            P(),
            P(),
            P("gx", "gy", "gz", None, None),
            P("gx", "gy", "gz", None),
        ),
        out_specs=(P("gx", "gy", "gz", None, None), P("gx", "gy", "gz", None, None, None)),
        check_vma=False,
    )
```

```python
import functools

import jax
import jax.numpy as jnp
from jax import lax
from jax.experimental import pallas as pl
from jax.experimental.pallas import tpu as pltpu
from jax.sharding import PartitionSpec as P

NODES = 125
FACE = 25
LANES = 128
COUNT = 256
SLOTS = 512
CAP = 16
GROUPS = 32
FACE_ROWS = 32
STACK = 6 * FACE_ROWS
MESH = pl.DeviceIdType.MESH
F32 = jnp.float32
BF16 = jnp.bfloat16
HIGHEST = lax.Precision.HIGHEST

HALO = ((0, 16), (16, 16), (32, 8), (40, 8), (48, 8), (56, 8))
HALO_ROWS = 64
DX = (4, 3, 5, 2, 6, 1, 7, 0)
ORDER = range(GROUPS - 1)


def iota(shape, dim):
    return lax.broadcasted_iota(jnp.int32, shape, dim)


def matmul(left, right):
    return lax.dot_general(
        left, right, (((1,), (0,)), ((), ())), preferred_element_type=F32
    )


def matmul_t(left, right):
    return lax.dot_general(
        left, right, (((1,), (1,)), ((), ())), preferred_element_type=F32
    )


def full(left, right):
    return lax.dot_general(
        left, right, (((1,), (0,)), ((), ())), precision=HIGHEST, preferred_element_type=F32
    )


def halves(values):
    high = values.astype(BF16)
    return high, (values - high.astype(F32)).astype(BF16)


def roll(values, shift):
    shift = shift % LANES
    return pltpu.roll(values, shift, 1) if shift else values


def face_rows():
    m = iota((FACE_ROWS, LANES), 0)
    node = iota((FACE_ROWS, LANES), 1)
    a = sum((m >= cut).astype(jnp.int32) for cut in (5, 10, 15, 20))
    b = m - 5 * a
    picks = (m, m + 100, 25 * a + b, 25 * a + b + 20, 5 * m, 5 * m + 4)
    faces = [jnp.where((node == pick) & (m < FACE), 1.0, 0.0) for pick in picks]
    return jnp.concatenate(faces, axis=0).astype(BF16)


def pieces(face):
    return [(r, t, face[8 * r : 8 * r + 8, LANES * t : LANES * t + LANES]) for r in range(4) for t in range(2)]


def total(terms):
    while len(terms) > 1:
        terms = [sum(terms[i : i + 2]) for i in range(0, len(terms), 2)]
    return terms[0]


def pack_halo(out, tx):
    lane = iota((8, LANES), 1)
    z, y = lane & 7, (lane >> 3) & 7
    low = lane < 64
    face = lambda f: out[FACE_ROWS * f : FACE_ROWS * (f + 1)]
    piece = {f: {(r, t): v for r, t, v in pieces(face(f))} for f in range(6)}
    for j in range(2):
        tx[8 * j : 8 * j + 8] = jnp.where(low, roll(piece[1][2 * j, 1], 64), piece[1][2 * j + 1, 1])
        tx[16 + 8 * j : 24 + 8 * j] = jnp.where(low, piece[0][2 * j, 0], roll(piece[0][2 * j + 1, 0], 64))

    def gather(f, keep, shift):
        return total([
            roll(jnp.where(keep, piece[f][r, t], 0.0), shift(2 * r + t)) for r in range(4) for t in range(2)
        ])

    tx[32:40] = gather(3, y == 7, lambda q: 8 * q - 56)
    tx[40:48] = gather(2, y == 0, lambda q: 8 * q)
    tx[48:56] = gather(5, z == 7, lambda q: q - 7)
    tx[56:64] = gather(4, z == 0, lambda q: q)


def shift_inside(out, inc):
    lane = iota((FACE_ROWS, LANES), 1)
    z, y = lane & 7, (lane >> 3) & 7
    low = lane < 64
    tile = lambda f, t: out[FACE_ROWS * f : FACE_ROWS * (f + 1), LANES * t : LANES * (t + 1)]

    def put(f, t, values):
        inc[t, FACE_ROWS * f : FACE_ROWS * (f + 1)] = values

    a, b = roll(tile(1, 0), 64), roll(tile(1, 1), 64)
    put(0, 0, jnp.where(low, 0.0, a))
    put(0, 1, jnp.where(low, a, b))
    a, b = roll(tile(0, 0), 64), roll(tile(0, 1), 64)
    put(1, 0, jnp.where(low, a, b))
    put(1, 1, jnp.where(low, b, 0.0))
    for t in range(2):
        put(2, t, jnp.where(y == 0, 0.0, roll(tile(3, t), 8)))
        put(3, t, jnp.where(y == 7, 0.0, roll(tile(2, t), -8)))
        put(4, t, jnp.where(z == 0, 0.0, roll(tile(5, t), 1)))
        put(5, t, jnp.where(z == 7, 0.0, roll(tile(4, t), -1)))


def add_halo(rx, inc, inner):
    lane = iota((8, LANES), 1)
    z, y = lane & 7, (lane >> 3) & 7
    low = lane < 64
    has = [jnp.full((8, LANES), inner[i ^ 1].astype(jnp.int32), jnp.int32) > 0 for i in range(6)]

    def add(f, r, t, keep, values):
        rows = slice(FACE_ROWS * f + 8 * r, FACE_ROWS * f + 8 * r + 8)
        inc[t, rows] = jnp.where(keep, values, inc[t, rows])

    for j in range(2):
        part = rx[8 * j : 8 * j + 8]
        add(0, 2 * j, 0, low & has[0], part)
        add(0, 2 * j + 1, 0, low & has[0], roll(part, 64))
        part = rx[16 + 8 * j : 24 + 8 * j]
        add(1, 2 * j, 1, (lane >= 64) & has[1], roll(part, 64))
        add(1, 2 * j + 1, 1, (lane >= 64) & has[1], part)
    for r in range(4):
        for t in range(2):
            q = 2 * r + t
            add(2, r, t, (y == 0) & has[2], roll(rx[32:40], -8 * q))
            add(3, r, t, (y == 7) & has[3], roll(rx[40:48], 56 - 8 * q))
            add(4, r, t, (z == 0) & has[4], roll(rx[48:56], -q))
            add(5, r, t, (z == 7) & has[5], roll(rx[56:64], 7 - q))


def kernel(
    source_hbm, stiffness_hbm, relax_hbm, owners_hbm, material_hbm,
    landed, inc,
    src, stiff, relax, owner, mat, kpad, rpad, packer, moved, tx, rx,
    in_sem, halo_send, halo_recv, move_send, move_recv, side_sem, ready_sem, first_sem, relay, relay_send, relay_recv,
):
    gx, gy, gz = (lax.axis_index(axis) for axis in ("gx", "gy", "gz"))
    loads = [
        pltpu.make_async_copy(stiffness_hbm, stiff, in_sem.at[0]),
        pltpu.make_async_copy(relax_hbm, relax, in_sem.at[1]),
        pltpu.make_async_copy(source_hbm.at[:, 0, pl.ds(0, LANES)], src.at[0, pl.ds(0, NODES)], in_sem.at[2]),
        pltpu.make_async_copy(source_hbm.at[:, 0, pl.ds(LANES, LANES)], src.at[1, pl.ds(0, NODES)], in_sem.at[5]),
        pltpu.make_async_copy(owners_hbm, owner, in_sem.at[3]),
        pltpu.make_async_copy(material_hbm, mat, in_sem.at[4]),
    ]
    for t in range(2):
        src[t, 120:128] = jnp.zeros((8, LANES), F32)
    for load in loads:
        load.start()
    rx[...] = jnp.zeros_like(rx)

    my_y, my_x, my_c = gx // 16, (gx // 2) % 8, gx % 2

    def number(flag):
        return flag.astype(jnp.int32)

    def peer_at(chunk):
        dx, dy, dc = DX[chunk // 4], 1 - chunk // 2 % 2, 1 - chunk % 2
        return (my_y + dy) % 2, (my_x + dx) % 8, (my_c + dc) % 2

    def peer(chunk):
        y, x, c = peer_at(chunk)
        return y * 16 + x * 2 + c

    def rank_of(y, x, c):
        return jnp.maximum(2 * jnp.minimum(x, 8 - x) - 1 + number(x > 4), 0) * 4 + y * 2 + 1 - c

    def rank_at(index):
        return rank_of(index // 16, (index // 2) % 8, index % 2)

    line0 = (gy == 0) & (gz == 0)
    last = line0 & (gx == 0)
    rank = rank_of(my_y, my_x, my_c)
    my_rank = rank + 32 * number(last)

    def is_later(chunk):
        y, x, c = peer_at(chunk)
        return rank_of(y, x, c) + 32 * number(line0 & (y + x + c == 0)) > my_rank

    earlier_peers = jnp.where(last, 31, rank - number(line0 & (rank > 1)))
    later_peers = jnp.where(last, 0, 31 - number(line0) - earlier_peers)

    sides = (
        (gx + 1, gy, gz), (gx - 1, gy, gz), (gx, gy + 1, gz), (gx, gy - 1, gz), (gx, gy, gz + 1), (gx, gy, gz - 1),
    )
    there = (gx < 31, gx > 0, gy < 3, gy > 0, gz < 7, gz > 0)
    no = gx < 0
    to_last = (
        no, (gx == 1) & line0, no, (gx == 0) & (gy == 1) & (gz == 0), no, (gx == 0) & (gy == 0) & (gz == 1),
    )
    usual = (rank_at(gx + 1) > rank, rank_at(gx - 1) > rank, gy < 2, gy == 3, gz >= 0, no)
    later = [there[i] & (to_last[i] | (jnp.logical_not(last) & usual[i])) for i in range(6)]
    earlier = [there[i] & jnp.logical_not(later[i]) for i in range(6)]
    greeted = earlier_peers + sum(number(earlier[i]) for i in range(2, 6)) + number(to_last[3] | to_last[5])

    def signal(semaphore, device):
        pl.semaphore_signal(semaphore, 1, device_id=device, device_id_type=MESH)

    barrier = pltpu.get_barrier_semaphore()
    for i in range(2, 6):
        pl.when(later[i])(functools.partial(signal, barrier, sides[i]))

    @pl.when(to_last[1])
    def _():
        signal(barrier, (0, 1, 0))
        signal(barrier, (0, 0, 1))

    @pl.when(jnp.logical_not(last))
    def _():
        for chunk in ORDER:
            pl.when(is_later(chunk))(functools.partial(signal, barrier, (peer(chunk), gy, gz)))

    def answer_sides():
        @pl.when(greeted > 0)
        def _():
            pl.semaphore_wait(barrier, greeted)

        for i in range(6):
            pl.when(earlier[i])(functools.partial(signal, side_sem.at[i ^ 1], sides[i]))

    @pl.when(last)
    def _():
        answer_sides()
        for chunk in ORDER:
            signal(first_sem, (peer(chunk), gy, gz))

    kpad[...] = jnp.zeros((LANES, LANES), F32)
    rpad[...] = jnp.zeros((8, LANES), F32)
    loads[0].wait()
    loads[1].wait()
    kpad[0:NODES, 0:NODES] = stiff[...]
    rpad[0:1, 0:NODES] = relax[...]
    eye = iota((LANES, LANES), 0) == iota((LANES, LANES), 1)
    row = jnp.broadcast_to(rpad[0:1], (LANES, LANES))
    diag = jnp.where(eye, row, 0.0)
    col = jnp.sum(diag, axis=1, keepdims=True)
    scaled = col * kpad[...]
    step = jnp.where(eye, 1.0, 0.0) - scaled
    sum2 = 2.0 * diag - scaled * row
    step2 = full(step, step)
    sum4 = sum2 + full(step2, sum2)
    step4 = full(step2, step2)
    sum8 = sum4 + full(step4, sum4)
    elastic_op, acoustic_op = sum8 * (1.0 / 3.0), sum2
    pl.when(jnp.logical_not(last))(answer_sides)

    for load in loads[2:]:
        load.wait()
    elastic = jnp.broadcast_to(mat[...], (LANES, COUNT)) > 0
    source = jnp.concatenate([src[0], src[1]], axis=1)
    field = jnp.where(elastic, full(elastic_op, source), full(acoustic_op, source))
    pick = face_rows()
    high, low = halves(field)
    faces = matmul(pick, high) + matmul(pick, low)
    out = 2.0 * faces
    pack_halo(out, tx.at[0])

    def halo_copy(step, i):
        at, rows = HALO[i]
        return pltpu.make_async_remote_copy(
            src_ref=tx.at[step, pl.ds(at, rows)],
            dst_ref=rx.at[step, pl.ds(at, rows)],
            send_sem=halo_send.at[step, i],
            recv_sem=halo_recv.at[step, i],
            device_id=sides[i],
            device_id_type=MESH,
        )

    def halo_start(step, i, when):
        @pl.when(when)
        def _():
            halo_copy(step, i).start()

    def halo_wait_recv(step):
        for i in range(6):
            @pl.when(there[i ^ 1])
            def _():
                halo_copy(step, i).wait_recv()

    def halo_wait_send(step):
        for i in range(6):
            @pl.when(there[i])
            def _():
                halo_copy(step, i).wait_send()

    for i in range(6):
        halo_start(0, i, earlier[i])

    @pl.when(jnp.logical_not(last))
    def _():
        for chunk in ORDER:
            pl.when(jnp.logical_not(is_later(chunk)))(
                functools.partial(signal, ready_sem, (peer(chunk), gy, gz))
            )

    def relay_in(i, k):
        at, rows = HALO[i]
        return pltpu.make_async_remote_copy(
            src_ref=tx.at[0, pl.ds(at, rows)],
            dst_ref=relay.at[pl.ds(8 * k, rows)],
            send_sem=halo_send.at[0, i],
            recv_sem=relay_recv.at[k],
            device_id=(1, 0, 0),
            device_id_type=MESH,
        )

    def relay_out(i, k):
        at, rows = HALO[i]
        return pltpu.make_async_remote_copy(
            src_ref=relay.at[pl.ds(8 * k, rows)],
            dst_ref=rx.at[0, pl.ds(at, rows)],
            send_sem=relay_send.at[k],
            recv_sem=halo_recv.at[0, i],
            device_id=(0, 0, 0),
            device_id_type=MESH,
        )

    for k, i in enumerate((3, 5)):
        pl.when(to_last[i])(lambda k=k, i=i: relay_in(i, k).start())

    def halo_start_later():
        for i in range(6):
            @pl.when(later[i] & jnp.logical_not(to_last[i]))
            def _():
                pl.semaphore_wait(side_sem.at[i], 1)
                halo_copy(0, i).start()

    halo_start_later()

    shift_inside(out, inc)
    ops = []
    for op in (elastic_op, acoustic_op):
        high, low = halves(op)
        nodes = matmul_t(high, pick) + matmul_t(low, pick)
        high, low = halves(nodes)
        ops.append((high, low))
    on_nodes = [jnp.concatenate([ops[0][i], ops[1][i]], axis=0) for i in range(2)]
    on_faces = [
        jnp.concatenate([matmul(pick, ops[0][i]), matmul(pick, ops[1][i])], axis=0).astype(BF16) for i in range(2)
    ]

    names = owner[...]
    named = iota((GROUPS, COUNT), 0) == jnp.broadcast_to(names, (GROUPS, COUNT))
    before = jnp.where(iota((COUNT, COUNT), 0) < iota((COUNT, COUNT), 1), 1.0, 0.0).astype(BF16)
    counts = matmul(jnp.where(named, 1.0, 0.0).astype(BF16), before)
    place = jnp.sum(jnp.where(named, counts, 0.0), axis=0, keepdims=True).astype(jnp.int32)
    ahead = ((names >> 1) - my_x) & 7
    near = jnp.minimum(ahead, 8 - ahead)
    ring = jnp.maximum(7 - 2 * near + jnp.where(ahead > 4, 1, 0), 0)
    chunk = 4 * ring + 2 * (1 - ((names >> 4) ^ my_y)) + 1 - ((names & 1) ^ my_c)
    slot = chunk * CAP + place
    for k in range(4):
        here = iota((LANES, COUNT), 0) + k * LANES == jnp.broadcast_to(slot, (LANES, COUNT))
        packer[k * LANES : (k + 1) * LANES] = jnp.where(here, 1.0, 0.0).astype(BF16)

    @pl.when(to_last[1])
    def _():
        pl.semaphore_wait(side_sem.at[1], 1)
        halo_copy(0, 1).start()
        for k, i in enumerate((3, 5)):
            relay_in(i, k).wait_recv()
            relay_out(i, k).start()

    halo_wait_recv(0)
    add_halo(rx.at[0], inc, there)

    incoming = jnp.concatenate([inc[0], inc[1]], axis=1)
    high, low = halves(incoming)

    def on_traces(op):
        return matmul(op[0], high) + matmul(op[0], low) + matmul(op[1], high)

    change = on_traces(on_nodes)
    field = field + jnp.where(elastic, change[0:LANES], change[LANES : 2 * LANES])
    both = jnp.concatenate(halves(field), axis=0)
    mine = pl.ds(pl.multiple_of(gx * CAP, CAP), CAP)

    def move(chunk, device=None):
        return pltpu.make_async_remote_copy(
            src_ref=moved.at[pl.ds(pl.multiple_of(chunk * CAP, CAP), CAP)],
            dst_ref=landed.at[mine],
            send_sem=move_send.at[chunk],
            recv_sem=move_recv.at[chunk],
            device_id=device or (peer(chunk), gy, gz),
            device_id_type=MESH,
        )

    @pl.when(later_peers > 0)
    def _():
        pl.semaphore_wait(ready_sem, later_peers)

    for k in range(4):
        part = matmul_t(packer[k * LANES : (k + 1) * LANES], both)
        moved[k * LANES : (k + 1) * LANES] = part[:, 0:LANES] + part[:, LANES : 2 * LANES]
        for chunk in ORDER[8 * k : 8 * k + 8]:
            pl.when(jnp.logical_not(line0 & (peer(chunk) == 0)))(lambda chunk=chunk: move(chunk).start())
    landed[mine] = moved[SLOTS - CAP : SLOTS]

    change = on_traces(on_faces)
    face_elastic = jnp.broadcast_to(mat[...], (STACK, COUNT)) > 0
    faces = faces + jnp.where(face_elastic, change[0:STACK], change[STACK : 2 * STACK])
    out = 2.0 * faces - incoming
    pack_halo(out, tx.at[1])
    for i in (3, 5):
        @pl.when(to_last[i])
        def _():
            pl.semaphore_wait(side_sem.at[i], 1)
    for i in range(6):
        halo_start(1, i, there[i])

    @pl.when(line0 & (gx > 0))
    def _():
        pl.semaphore_wait(first_sem, 1)
        ahead = (8 - my_x) % 8
        ring = jnp.maximum(7 - 2 * jnp.minimum(ahead, 8 - ahead) + number(ahead > 4), 0)
        move(4 * ring + 2 * (1 - my_y) + 1 - my_c, (0, gy, gz)).start()

    shift_inside(out, inc)
    halo_wait_recv(1)
    add_halo(rx.at[1], inc, there)
    for chunk in ORDER:
        move(chunk).wait_recv()
    halo_wait_send(0)
    halo_wait_send(1)

    @pl.when(to_last[1])
    def _():
        for k, i in enumerate((3, 5)):
            relay_out(i, k).wait_send()

    for chunk in ORDER:
        move(chunk).wait_send()


def finish(landed, inc, settled_hbm, incoming_hbm, turned, out_sem):
    results = []
    for f in range(6):
        for t in range(2):
            results.append(
                pltpu.make_async_copy(
                    inc.at[t, pl.ds(f * FACE_ROWS, FACE)],
                    incoming_hbm.at[f, :, 0, pl.ds(t * LANES, LANES)],
                    out_sem.at[2 * f + t],
                )
            )
            results[-1].start()
    for k in range(4):
        turned[k] = landed[k * LANES : (k + 1) * LANES].T
        results.append(
            pltpu.make_async_copy(
                turned.at[k, pl.ds(0, NODES)], settled_hbm.at[:, 0, pl.ds(k * LANES, LANES)], out_sem.at[12 + k]
            )
        )
        results[-1].start()
    for copy in results:
        copy.wait()


def shards(source, stiffness, relax, owners, material):
    anywhere = pl.BlockSpec(memory_space=pl.ANY)
    vmem = pl.BlockSpec(memory_space=pltpu.VMEM)
    operands = (
        source.reshape(NODES, 1, COUNT),
        stiffness,
        relax.reshape(1, NODES),
        owners.reshape(1, COUNT),
        material.reshape(1, COUNT),
    )
    landed, inc = pl.pallas_call(
        kernel,
        out_shape=(pltpu.VMEM((SLOTS, LANES), F32), pltpu.VMEM((2, STACK, LANES), F32)),
        in_specs=[anywhere] * 5,
        out_specs=(vmem, vmem),
        scratch_shapes=[
            pltpu.VMEM((2, LANES, LANES), F32),
            pltpu.VMEM((NODES, NODES), F32),
            pltpu.VMEM((1, NODES), F32),
            pltpu.VMEM((1, COUNT), jnp.int32),
            pltpu.VMEM((1, COUNT), jnp.int32),
            pltpu.VMEM((LANES, LANES), F32),
            pltpu.VMEM((8, LANES), F32),
            pltpu.VMEM((SLOTS, COUNT), BF16),
            pltpu.VMEM((SLOTS, LANES), F32),
            pltpu.VMEM((2, HALO_ROWS, LANES), F32),
            pltpu.VMEM((2, HALO_ROWS, LANES), F32),
            pltpu.SemaphoreType.DMA((6,)),
            pltpu.SemaphoreType.DMA((2, 6)),
            pltpu.SemaphoreType.DMA((2, 6)),
            pltpu.SemaphoreType.DMA((GROUPS,)),
            pltpu.SemaphoreType.DMA((GROUPS,)),
            pltpu.SemaphoreType.REGULAR((6,)),
            pltpu.SemaphoreType.REGULAR,
            pltpu.SemaphoreType.REGULAR,
            pltpu.VMEM((16, LANES), F32),
            pltpu.SemaphoreType.DMA((2,)),
            pltpu.SemaphoreType.DMA((2,)),
        ],
        compiler_params=pltpu.CompilerParams(
            collective_id=0, has_side_effects=True, vmem_limit_bytes=32 * 1024 * 1024
        ),
    )(*(pltpu.with_memory_space_constraint(x, pltpu.HBM) for x in operands))
    settled, incoming = pl.pallas_call(
        finish,
        out_shape=(pltpu.HBM((NODES, 1, SLOTS), F32), pltpu.HBM((6, FACE, 1, COUNT), F32)),
        in_specs=(vmem, vmem),
        out_specs=(anywhere, anywhere),
        scratch_shapes=[pltpu.VMEM((4, LANES, LANES), F32), pltpu.SemaphoreType.DMA((16,))],
        compiler_params=pltpu.CompilerParams(vmem_limit_bytes=32 * 1024 * 1024),
    )(landed, inc)
    return (
        settled.reshape(1, 1, 1, NODES, SLOTS),
        incoming.reshape(1, 1, 1, 6, FACE, COUNT),
    )


def solution(mesh):
    return jax.shard_map(
        shards,
        mesh=mesh,
        in_specs=(
            P("gx", "gy", "gz", None, None),
            P(),
            P(),
            P("gx", "gy", "gz", None, None),
            P("gx", "gy", "gz", None),
        ),
        out_specs=(P("gx", "gy", "gz", None, None), P("gx", "gy", "gz", None, None, None)),
        check_vma=False,
    )
```

```python
import functools

import jax
import jax.numpy as jnp
from jax import lax
from jax.experimental import pallas as pl
from jax.experimental.pallas import tpu as pltpu
from jax.sharding import PartitionSpec as P

NODES = 125
FACE = 25
LANES = 128
COUNT = 256
SLOTS = 512
CAP = 16
GROUPS = 32
FACE_ROWS = 32
STACK = 6 * FACE_ROWS
MESH = pl.DeviceIdType.MESH
F32 = jnp.float32
BF16 = jnp.bfloat16
HIGHEST = lax.Precision.HIGHEST

HALO = ((0, 16), (16, 16), (32, 8), (40, 8), (48, 8), (56, 8))
HALO_ROWS = 64
DX = (4, 3, 5, 2, 6, 1, 7, 0)
ORDER = range(GROUPS - 1)
LATE_ORDER = (20, 24, 21, 25, 22, 26, 23, 27, 30, 12, 16, 13, 17, 14, 18, 15, 19, 0, 8, 1, 9, 2, 10, 3, 11, 28, 29)


def iota(shape, dim):
    return lax.broadcasted_iota(jnp.int32, shape, dim)


def matmul(left, right):
    return lax.dot_general(
        left, right, (((1,), (0,)), ((), ())), preferred_element_type=F32
    )


def matmul_t(left, right):
    return lax.dot_general(
        left, right, (((1,), (1,)), ((), ())), preferred_element_type=F32
    )


def full(left, right):
    return lax.dot_general(
        left, right, (((1,), (0,)), ((), ())), precision=lax.Precision.HIGH, preferred_element_type=F32
    )


def halves(values):
    high = values.astype(BF16)
    return high, (values - high.astype(F32)).astype(BF16)


def roll(values, shift):
    shift = shift % LANES
    return pltpu.roll(values, shift, 1) if shift else values


def face_rows():
    m = iota((FACE_ROWS, LANES), 0)
    node = iota((FACE_ROWS, LANES), 1)
    a = sum((m >= cut).astype(jnp.int32) for cut in (5, 10, 15, 20))
    b = m - 5 * a
    picks = (m, m + 100, 25 * a + b, 25 * a + b + 20, 5 * m, 5 * m + 4)
    faces = [jnp.where((node == pick) & (m < FACE), 1.0, 0.0) for pick in picks]
    return jnp.concatenate(faces, axis=0).astype(BF16)


def pieces(face):
    return [(r, t, face[8 * r : 8 * r + 8, LANES * t : LANES * t + LANES]) for r in range(4) for t in range(2)]


def total(terms):
    while len(terms) > 1:
        terms = [sum(terms[i : i + 2]) for i in range(0, len(terms), 2)]
    return terms[0]


def pack_halo(out, tx):
    lane = iota((8, LANES), 1)
    z, y = lane & 7, (lane >> 3) & 7
    low = lane < 64
    face = lambda f: out[FACE_ROWS * f : FACE_ROWS * (f + 1)]
    piece = {f: {(r, t): v for r, t, v in pieces(face(f))} for f in range(6)}
    for j in range(2):
        tx[8 * j : 8 * j + 8] = jnp.where(low, roll(piece[1][2 * j, 1], 64), piece[1][2 * j + 1, 1])
        tx[16 + 8 * j : 24 + 8 * j] = jnp.where(low, piece[0][2 * j, 0], roll(piece[0][2 * j + 1, 0], 64))

    def gather(f, keep, shift):
        return total([
            roll(jnp.where(keep, piece[f][r, t], 0.0), shift(2 * r + t)) for r in range(4) for t in range(2)
        ])

    tx[32:40] = gather(3, y == 7, lambda q: 8 * q - 56)
    tx[40:48] = gather(2, y == 0, lambda q: 8 * q)
    tx[48:56] = gather(5, z == 7, lambda q: q - 7)
    tx[56:64] = gather(4, z == 0, lambda q: q)


def shift_inside(out, inc):
    lane = iota((FACE_ROWS, LANES), 1)
    z, y = lane & 7, (lane >> 3) & 7
    low = lane < 64
    tile = lambda f, t: out[FACE_ROWS * f : FACE_ROWS * (f + 1), LANES * t : LANES * (t + 1)]

    def put(f, t, values):
        inc[t, FACE_ROWS * f : FACE_ROWS * (f + 1)] = values

    a, b = roll(tile(1, 0), 64), roll(tile(1, 1), 64)
    put(0, 0, jnp.where(low, 0.0, a))
    put(0, 1, jnp.where(low, a, b))
    a, b = roll(tile(0, 0), 64), roll(tile(0, 1), 64)
    put(1, 0, jnp.where(low, a, b))
    put(1, 1, jnp.where(low, b, 0.0))
    for t in range(2):
        put(2, t, jnp.where(y == 0, 0.0, roll(tile(3, t), 8)))
        put(3, t, jnp.where(y == 7, 0.0, roll(tile(2, t), -8)))
        put(4, t, jnp.where(z == 0, 0.0, roll(tile(5, t), 1)))
        put(5, t, jnp.where(z == 7, 0.0, roll(tile(4, t), -1)))


def add_halo(rx, inc, inner):
    lane = iota((8, LANES), 1)
    z, y = lane & 7, (lane >> 3) & 7
    low = lane < 64
    has = [jnp.full((8, LANES), inner[i ^ 1].astype(jnp.int32), jnp.int32) > 0 for i in range(6)]

    def add(f, r, t, keep, values):
        rows = slice(FACE_ROWS * f + 8 * r, FACE_ROWS * f + 8 * r + 8)
        inc[t, rows] = jnp.where(keep, values, inc[t, rows])

    for j in range(2):
        part = rx[8 * j : 8 * j + 8]
        add(0, 2 * j, 0, low & has[0], part)
        add(0, 2 * j + 1, 0, low & has[0], roll(part, 64))
        part = rx[16 + 8 * j : 24 + 8 * j]
        add(1, 2 * j, 1, (lane >= 64) & has[1], roll(part, 64))
        add(1, 2 * j + 1, 1, (lane >= 64) & has[1], part)
    for r in range(4):
        for t in range(2):
            q = 2 * r + t
            add(2, r, t, (y == 0) & has[2], roll(rx[32:40], -8 * q))
            add(3, r, t, (y == 7) & has[3], roll(rx[40:48], 56 - 8 * q))
            add(4, r, t, (z == 0) & has[4], roll(rx[48:56], -q))
            add(5, r, t, (z == 7) & has[5], roll(rx[56:64], 7 - q))


def kernel(
    source_hbm, stiffness_hbm, relax_hbm, owners_hbm, material_hbm,
    landed, inc,
    src, stiff, relax, owner, mat, kpad, rpad, packer, moved, tx, rx,
    in_sem, halo_send, halo_recv, move_send, move_recv, side_sem, ready_sem, first_sem, relay, relay_send, relay_recv, nodes, picked,
):
    gx, gy, gz = (lax.axis_index(axis) for axis in ("gx", "gy", "gz"))
    loads = [
        *(
            pltpu.make_async_copy(stiffness_hbm.at[pl.ds(at, rows)], stiff.at[pl.ds(at, rows)], in_sem.at[6 + k])
            for k, (at, rows) in enumerate(((0, 32), (32, 32), (64, 32), (96, 29)))
        ),
        pltpu.make_async_copy(relax_hbm, relax, in_sem.at[1]),
        pltpu.make_async_copy(source_hbm.at[:, 0, pl.ds(0, LANES)], src.at[0, pl.ds(0, NODES)], in_sem.at[2]),
        pltpu.make_async_copy(source_hbm.at[:, 0, pl.ds(LANES, LANES)], src.at[1, pl.ds(0, NODES)], in_sem.at[5]),
        pltpu.make_async_copy(owners_hbm, owner, in_sem.at[3]),
        pltpu.make_async_copy(material_hbm, mat, in_sem.at[4]),
    ]
    for t in range(2):
        src[t, 120:128] = jnp.zeros((8, LANES), F32)
    for load in loads:
        load.start()
    rx[...] = jnp.zeros_like(rx)
    picked[...] = jnp.zeros_like(picked)

    my_y, my_x, my_c = gx // 16, (gx // 2) % 8, gx % 2

    def number(flag):
        return flag.astype(jnp.int32)

    def peer_at(chunk):
        dx, dy, dc = DX[chunk // 4], 1 - chunk // 2 % 2, 1 - chunk % 2
        return (my_y + dy) % 2, (my_x + dx) % 8, (my_c + dc) % 2

    def peer(chunk):
        y, x, c = peer_at(chunk)
        return y * 16 + x * 2 + c

    def rank_of(y, x, c):
        return jnp.maximum(2 * jnp.minimum(x, 8 - x) - 1 + number(x > 4), 0) * 4 + y * 2 + 1 - c

    def rank_at(index):
        return rank_of(index // 16, (index // 2) % 8, index % 2)

    line0 = (gy == 0) & (gz == 0)
    last = line0 & (gx == 0)
    rank = rank_of(my_y, my_x, my_c)
    my_rank = rank + 32 * number(last)

    def is_later(chunk):
        y, x, c = peer_at(chunk)
        return rank_of(y, x, c) + 32 * number(line0 & (y + x + c == 0)) > my_rank

    earlier_peers = jnp.where(last, 31, rank - number(line0 & (rank > 1)))
    later_peers = jnp.where(last, 0, 31 - number(line0) - earlier_peers)

    sides = (
        (gx + 1, gy, gz), (gx - 1, gy, gz), (gx, gy + 1, gz), (gx, gy - 1, gz), (gx, gy, gz + 1), (gx, gy, gz - 1),
    )
    there = (gx < 31, gx > 0, gy < 3, gy > 0, gz < 7, gz > 0)
    no = gx < 0
    to_last = (
        no, (gx == 1) & line0, no, (gx == 0) & (gy == 1) & (gz == 0), no, (gx == 0) & (gy == 0) & (gz == 1),
    )
    slow = last | to_last[1] | to_last[3] | to_last[5]
    usual = (rank_at(gx + 1) > rank, rank_at(gx - 1) > rank, gy < 2, gy == 3, gz >= 0, no)
    later = [there[i] & (to_last[i] | (jnp.logical_not(last) & usual[i])) for i in range(6)]
    earlier = [there[i] & jnp.logical_not(later[i]) for i in range(6)]
    greeted = earlier_peers + sum(number(earlier[i]) for i in range(2, 6)) + number(to_last[3] | to_last[5])

    def signal(semaphore, device):
        pl.semaphore_signal(semaphore, 1, device_id=device, device_id_type=MESH)

    barrier = pltpu.get_barrier_semaphore()
    for i in range(2, 6):
        pl.when(later[i])(functools.partial(signal, barrier, sides[i]))

    @pl.when(to_last[1])
    def _():
        signal(barrier, (0, 1, 0))
        signal(barrier, (0, 0, 1))

    @pl.when(jnp.logical_not(last))
    def _():
        for chunk in ORDER:
            pl.when(is_later(chunk))(functools.partial(signal, barrier, (peer(chunk), gy, gz)))

    def answer_sides():
        @pl.when(greeted > 0)
        def _():
            pl.semaphore_wait(barrier, greeted)

        for i in range(6):
            pl.when(earlier[i])(functools.partial(signal, side_sem.at[i ^ 1], sides[i]))

    @pl.when(last)
    def _():
        answer_sides()
        for chunk in ORDER:
            signal(first_sem, (peer(chunk), gy, gz))

    kpad[...] = jnp.zeros((LANES, LANES), F32)
    rpad[...] = jnp.zeros((8, LANES), F32)
    for load in loads[:5]:
        load.wait()
    kpad[0:NODES, 0:NODES] = stiff[...]
    rpad[0:1, 0:NODES] = relax[...]
    eye = iota((LANES, LANES), 0) == iota((LANES, LANES), 1)
    row = jnp.broadcast_to(rpad[0:1], (LANES, LANES))
    diag = jnp.where(eye, row, 0.0)
    col = jnp.sum(diag, axis=1, keepdims=True)
    scaled = col * kpad[...]
    step = jnp.where(eye, 1.0, 0.0) - scaled
    sum2 = 2.0 * diag - scaled * row
    step2 = full(step, step)
    sum4 = sum2 + full(step2, sum2)
    step4 = full(step2, step2)
    sum8 = sum4 + full(step4, sum4)
    elastic_op, acoustic_op = sum8 * (1.0 / 3.0), sum2

    for load in loads[5:]:
        load.wait()
    elastic = jnp.broadcast_to(mat[...], (LANES, COUNT)) > 0
    source = jnp.concatenate([src[0], src[1]], axis=1)
    field = jnp.where(elastic, full(elastic_op, source), full(acoustic_op, source))
    pick = face_rows()
    for t in range(2):
        nodes[t, 0:LANES] = field[:, LANES * t : LANES * (t + 1)]
        for f, (first, stride) in ((0, (0, 1)), (1, (100, 1)), (4, (0, 5)), (5, (4, 5))):
            picked[t, FACE_ROWS * f : FACE_ROWS * f + FACE] = nodes[t, pl.ds(first, FACE, stride=stride)]
        for f, first in ((2, 0), (3, 20)):
            for a in range(5):
                at = FACE_ROWS * f + 5 * a
                picked[t, at : at + 5] = nodes[t, 25 * a + first : 25 * a + first + 5]
    faces = jnp.concatenate([picked[0], picked[1]], axis=1)
    out = 2.0 * faces
    pack_halo(out, tx.at[0])

    def halo_copy(step, i):
        at, rows = HALO[i]
        return pltpu.make_async_remote_copy(
            src_ref=tx.at[step, pl.ds(at, rows)],
            dst_ref=rx.at[step, pl.ds(at, rows)],
            send_sem=halo_send.at[step, i],
            recv_sem=halo_recv.at[step, i],
            device_id=sides[i],
            device_id_type=MESH,
        )

    def halo_start(step, i, when):
        @pl.when(when)
        def _():
            halo_copy(step, i).start()

    def halo_wait_recv(step):
        for i in range(6):
            @pl.when(there[i ^ 1])
            def _():
                halo_copy(step, i).wait_recv()

    def halo_wait_send(step):
        for i in range(6):
            @pl.when(there[i])
            def _():
                halo_copy(step, i).wait_send()

    pl.when(jnp.logical_not(last))(answer_sides)

    for i in range(6):
        halo_start(0, i, earlier[i])

    @pl.when(jnp.logical_not(last))
    def _():
        for chunk in ORDER:
            pl.when(jnp.logical_not(is_later(chunk)))(
                functools.partial(signal, ready_sem, (peer(chunk), gy, gz))
            )

    def relay_in(i, k):
        at, rows = HALO[i]
        return pltpu.make_async_remote_copy(
            src_ref=tx.at[0, pl.ds(at, rows)],
            dst_ref=relay.at[pl.ds(8 * k, rows)],
            send_sem=halo_send.at[0, i],
            recv_sem=relay_recv.at[k],
            device_id=(1, 0, 0),
            device_id_type=MESH,
        )

    def relay_out(i, k):
        at, rows = HALO[i]
        return pltpu.make_async_remote_copy(
            src_ref=relay.at[pl.ds(8 * k, rows)],
            dst_ref=rx.at[0, pl.ds(at, rows)],
            send_sem=relay_send.at[k],
            recv_sem=halo_recv.at[0, i],
            device_id=(0, 0, 0),
            device_id_type=MESH,
        )

    for k, i in enumerate((3, 5)):
        pl.when(to_last[i])(lambda k=k, i=i: relay_in(i, k).start())

    def halo_start_later():
        for i in range(6):
            @pl.when(later[i] & jnp.logical_not(to_last[i]))
            def _():
                pl.semaphore_wait(side_sem.at[i], 1)
                halo_copy(0, i).start()

    halo_start_later()

    shift_inside(out, inc)
    ops = []
    for op in (elastic_op, acoustic_op):
        high, low = halves(op)
        nodes = matmul_t(high, pick) + matmul_t(low, pick)
        high, low = halves(nodes)
        ops.append((high, low))
    on_nodes = [jnp.concatenate([ops[0][i], ops[1][i]], axis=0) for i in range(2)]
    on_faces = [
        jnp.concatenate([matmul(pick, ops[0][i]), matmul(pick, ops[1][i])], axis=0).astype(BF16) for i in range(2)
    ]

    names = owner[...]
    named = iota((GROUPS, COUNT), 0) == jnp.broadcast_to(names, (GROUPS, COUNT))
    before = jnp.where(iota((COUNT, COUNT), 0) < iota((COUNT, COUNT), 1), 1.0, 0.0).astype(BF16)
    counts = matmul(jnp.where(named, 1.0, 0.0).astype(BF16), before)
    place = jnp.sum(jnp.where(named, counts, 0.0), axis=0, keepdims=True).astype(jnp.int32)
    ahead = ((names >> 1) - my_x) & 7
    near = jnp.minimum(ahead, 8 - ahead)
    ring = jnp.maximum(7 - 2 * near + jnp.where(ahead > 4, 1, 0), 0)
    chunk = 4 * ring + 2 * (1 - ((names >> 4) ^ my_y)) + 1 - ((names & 1) ^ my_c)
    slot = chunk * CAP + place
    for k in range(4):
        here = iota((LANES, COUNT), 0) + k * LANES == jnp.broadcast_to(slot, (LANES, COUNT))
        packer[k * LANES : (k + 1) * LANES] = jnp.where(here, 1.0, 0.0).astype(BF16)

    @pl.when(to_last[1])
    def _():
        pl.semaphore_wait(side_sem.at[1], 1)
        halo_copy(0, 1).start()
        for k, i in enumerate((3, 5)):
            relay_in(i, k).wait_recv()
            relay_out(i, k).start()

    halo_wait_recv(0)
    add_halo(rx.at[0], inc, there)

    incoming = jnp.concatenate([inc[0], inc[1]], axis=1)
    high, low = halves(incoming)

    def on_traces(op):
        return matmul(op[0], high) + matmul(op[0], low) + matmul(op[1], high)

    change = on_traces(on_nodes)
    field = field + jnp.where(elastic, change[0:LANES], change[LANES : 2 * LANES])
    both = jnp.concatenate(halves(field), axis=0)
    mine = pl.ds(pl.multiple_of(gx * CAP, CAP), CAP)

    def move(chunk, device=None):
        return pltpu.make_async_remote_copy(
            src_ref=moved.at[pl.ds(pl.multiple_of(chunk * CAP, CAP), CAP)],
            dst_ref=landed.at[mine],
            send_sem=move_send.at[chunk],
            recv_sem=move_recv.at[chunk],
            device_id=device or (peer(chunk), gy, gz),
            device_id_type=MESH,
        )

    @pl.when(later_peers > 0)
    def _():
        pl.semaphore_wait(ready_sem, later_peers)

    for k in range(4):
        part = matmul_t(packer[k * LANES : (k + 1) * LANES], both)
        moved[k * LANES : (k + 1) * LANES] = part[:, 0:LANES] + part[:, LANES : 2 * LANES]
        for chunk in ORDER[8 * k : 8 * k + 8]:
            held = line0 & (peer(chunk) == 0)
            held = held if chunk // 4 == 1 else held | slow
            pl.when(jnp.logical_not(held))(lambda chunk=chunk: move(chunk).start())
    landed[mine] = moved[SLOTS - CAP : SLOTS]

    change = on_traces(on_faces)
    face_elastic = jnp.broadcast_to(mat[...], (STACK, COUNT)) > 0
    faces = faces + jnp.where(face_elastic, change[0:STACK], change[STACK : 2 * STACK])
    out = 2.0 * faces - incoming
    pack_halo(out, tx.at[1])
    for i in (3, 5):
        @pl.when(to_last[i])
        def _():
            pl.semaphore_wait(side_sem.at[i], 1)
    for i in range(6):
        halo_start(1, i, there[i])

    @pl.when(slow)
    def _():
        for chunk in LATE_ORDER:
            pl.when(jnp.logical_not(line0 & (peer(chunk) == 0)))(lambda chunk=chunk: move(chunk).start())

    @pl.when(line0 & (gx > 0))
    def _():
        pl.semaphore_wait(first_sem, 1)
        ahead = (8 - my_x) % 8
        ring = jnp.maximum(7 - 2 * jnp.minimum(ahead, 8 - ahead) + number(ahead > 4), 0)
        move(4 * ring + 2 * (1 - my_y) + 1 - my_c, (0, gy, gz)).start()

    shift_inside(out, inc)
    halo_wait_recv(1)
    add_halo(rx.at[1], inc, there)
    for chunk in ORDER:
        move(chunk).wait_recv()
    halo_wait_send(0)
    halo_wait_send(1)

    @pl.when(to_last[1])
    def _():
        for k, i in enumerate((3, 5)):
            relay_out(i, k).wait_send()

    for chunk in ORDER:
        move(chunk).wait_send()


def finish(landed, inc, settled_hbm, incoming_hbm, turned, out_sem):
    results = []
    for k in range(4):
        turned[k] = landed[k * LANES : (k + 1) * LANES].T
        results.append(
            pltpu.make_async_copy(
                turned.at[k, pl.ds(0, NODES)], settled_hbm.at[:, 0, pl.ds(k * LANES, LANES)], out_sem.at[2 + k]
            )
        )
        results[-1].start()
    for t in range(2):
        results.append(
            pltpu.make_async_copy(
                inc.at[t, :, pl.ds(0, FACE)], incoming_hbm.at[:, :, 0, pl.ds(t * LANES, LANES)], out_sem.at[t]
            )
        )
        results[-1].start()
    for copy in results:
        copy.wait()


def shards(source, stiffness, relax, owners, material):
    anywhere = pl.BlockSpec(memory_space=pl.ANY)
    vmem = pl.BlockSpec(memory_space=pltpu.VMEM)
    operands = (
        source.reshape(NODES, 1, COUNT),
        stiffness,
        relax.reshape(1, NODES),
        owners.reshape(1, COUNT),
        material.reshape(1, COUNT),
    )
    landed, inc = pl.pallas_call(
        kernel,
        out_shape=(pltpu.VMEM((SLOTS, LANES), F32), pltpu.VMEM((2, STACK, LANES), F32)),
        in_specs=[anywhere] * 5,
        out_specs=(vmem, vmem),
        scratch_shapes=[
            pltpu.VMEM((2, LANES, LANES), F32),
            pltpu.VMEM((NODES, NODES), F32),
            pltpu.VMEM((1, NODES), F32),
            pltpu.VMEM((1, COUNT), jnp.int32),
            pltpu.VMEM((1, COUNT), jnp.int32),
            pltpu.VMEM((LANES, LANES), F32),
            pltpu.VMEM((8, LANES), F32),
            pltpu.VMEM((SLOTS, COUNT), BF16),
            pltpu.VMEM((SLOTS, LANES), F32),
            pltpu.VMEM((2, HALO_ROWS, LANES), F32),
            pltpu.VMEM((2, HALO_ROWS, LANES), F32),
            pltpu.SemaphoreType.DMA((10,)),
            pltpu.SemaphoreType.DMA((2, 6)),
            pltpu.SemaphoreType.DMA((2, 6)),
            pltpu.SemaphoreType.DMA((GROUPS,)),
            pltpu.SemaphoreType.DMA((GROUPS,)),
            pltpu.SemaphoreType.REGULAR((6,)),
            pltpu.SemaphoreType.REGULAR,
            pltpu.SemaphoreType.REGULAR,
            pltpu.VMEM((16, LANES), F32),
            pltpu.SemaphoreType.DMA((2,)),
            pltpu.SemaphoreType.DMA((2,)),
            pltpu.VMEM((2, LANES + 8, LANES), F32),
            pltpu.VMEM((2, STACK, LANES), F32),
        ],
        compiler_params=pltpu.CompilerParams(
            collective_id=0, has_side_effects=True, vmem_limit_bytes=32 * 1024 * 1024
        ),
    )(*(pltpu.with_memory_space_constraint(x, pltpu.HBM) for x in operands))
    settled, incoming = pl.pallas_call(
        finish,
        out_shape=(pltpu.HBM((NODES, 1, SLOTS), F32), pltpu.HBM((6, FACE, 1, COUNT), F32)),
        in_specs=(vmem, vmem),
        out_specs=(anywhere, anywhere),
        scratch_shapes=[pltpu.VMEM((4, LANES, LANES), F32), pltpu.SemaphoreType.DMA((6,))],
        compiler_params=pltpu.CompilerParams(vmem_limit_bytes=32 * 1024 * 1024),
    )(landed, inc.reshape(2, 6, FACE_ROWS, LANES))
    return (
        settled.reshape(1, 1, 1, NODES, SLOTS),
        incoming.reshape(1, 1, 1, 6, FACE, COUNT),
    )


def solution(mesh):
    return jax.shard_map(
        shards,
        mesh=mesh,
        in_specs=(
            P("gx", "gy", "gz", None, None),
            P(),
            P(),
            P("gx", "gy", "gz", None, None),
            P("gx", "gy", "gz", None),
        ),
        out_specs=(P("gx", "gy", "gz", None, None), P("gx", "gy", "gz", None, None, None)),
        check_vma=False,
    )
```

```python
import functools

import jax
import jax.numpy as jnp
from jax import lax
from jax.experimental import pallas as pl
from jax.experimental.pallas import tpu as pltpu
from jax.sharding import PartitionSpec as P

NODES = 125
FACE = 25
LANES = 128
COUNT = 256
SLOTS = 512
CAP = 16
GROUPS = 32
FACE_ROWS = 32
STACK = 6 * FACE_ROWS
MESH = pl.DeviceIdType.MESH
F32 = jnp.float32
BF16 = jnp.bfloat16
HIGHEST = lax.Precision.HIGHEST

HALO = ((0, 16), (16, 16), (32, 8), (40, 8), (48, 8), (56, 8))
HALO_ROWS = 64
DX = (4, 3, 5, 2, 6, 1, 7, 0)
ORDER = range(GROUPS - 1)
LATE_ORDER = (20, 24, 21, 25, 22, 26, 23, 27, 30, 12, 16, 13, 17, 14, 18, 15, 19, 0, 8, 1, 9, 2, 10, 3, 11, 28, 29)


def iota(shape, dim):
    return lax.broadcasted_iota(jnp.int32, shape, dim)


def matmul(left, right):
    return lax.dot_general(
        left, right, (((1,), (0,)), ((), ())), preferred_element_type=F32
    )


def matmul_t(left, right):
    return lax.dot_general(
        left, right, (((1,), (1,)), ((), ())), preferred_element_type=F32
    )


def full(left, right):
    return lax.dot_general(
        left, right, (((1,), (0,)), ((), ())), precision=lax.Precision.HIGH, preferred_element_type=F32
    )


def halves(values):
    high = values.astype(BF16)
    return high, (values - high.astype(F32)).astype(BF16)


def roll(values, shift):
    shift = shift % LANES
    return pltpu.roll(values, shift, 1) if shift else values


def face_rows():
    m = iota((FACE_ROWS, LANES), 0)
    node = iota((FACE_ROWS, LANES), 1)
    a = sum((m >= cut).astype(jnp.int32) for cut in (5, 10, 15, 20))
    b = m - 5 * a
    picks = (m, m + 100, 25 * a + b, 25 * a + b + 20, 5 * m, 5 * m + 4)
    faces = [jnp.where((node == pick) & (m < FACE), 1.0, 0.0) for pick in picks]
    return jnp.concatenate(faces, axis=0).astype(BF16)


def pieces(face):
    return [(r, t, face[8 * r : 8 * r + 8, LANES * t : LANES * t + LANES]) for r in range(4) for t in range(2)]


def total(terms):
    while len(terms) > 1:
        terms = [sum(terms[i : i + 2]) for i in range(0, len(terms), 2)]
    return terms[0]


def pack_halo(out, tx):
    lane = iota((8, LANES), 1)
    z, y = lane & 7, (lane >> 3) & 7
    low = lane < 64
    face = lambda f: out[FACE_ROWS * f : FACE_ROWS * (f + 1)]
    piece = {f: {(r, t): v for r, t, v in pieces(face(f))} for f in range(6)}
    for j in range(2):
        tx[8 * j : 8 * j + 8] = jnp.where(low, roll(piece[1][2 * j, 1], 64), piece[1][2 * j + 1, 1])
        tx[16 + 8 * j : 24 + 8 * j] = jnp.where(low, piece[0][2 * j, 0], roll(piece[0][2 * j + 1, 0], 64))

    def gather(f, keep, shift):
        return total([
            roll(jnp.where(keep, piece[f][r, t], 0.0), shift(2 * r + t)) for r in range(4) for t in range(2)
        ])

    tx[32:40] = gather(3, y == 7, lambda q: 8 * q - 56)
    tx[40:48] = gather(2, y == 0, lambda q: 8 * q)
    tx[48:56] = gather(5, z == 7, lambda q: q - 7)
    tx[56:64] = gather(4, z == 0, lambda q: q)


def shift_inside(out, inc):
    lane = iota((FACE_ROWS, LANES), 1)
    z, y = lane & 7, (lane >> 3) & 7
    low = lane < 64
    tile = lambda f, t: out[FACE_ROWS * f : FACE_ROWS * (f + 1), LANES * t : LANES * (t + 1)]

    def put(f, t, values):
        inc[t, FACE_ROWS * f : FACE_ROWS * (f + 1)] = values

    a, b = roll(tile(1, 0), 64), roll(tile(1, 1), 64)
    put(0, 0, jnp.where(low, 0.0, a))
    put(0, 1, jnp.where(low, a, b))
    a, b = roll(tile(0, 0), 64), roll(tile(0, 1), 64)
    put(1, 0, jnp.where(low, a, b))
    put(1, 1, jnp.where(low, b, 0.0))
    for t in range(2):
        put(2, t, jnp.where(y == 0, 0.0, roll(tile(3, t), 8)))
        put(3, t, jnp.where(y == 7, 0.0, roll(tile(2, t), -8)))
        put(4, t, jnp.where(z == 0, 0.0, roll(tile(5, t), 1)))
        put(5, t, jnp.where(z == 7, 0.0, roll(tile(4, t), -1)))


def add_halo(rx, inc, inner):
    lane = iota((8, LANES), 1)
    z, y = lane & 7, (lane >> 3) & 7
    low = lane < 64
    has = [jnp.full((8, LANES), inner[i ^ 1].astype(jnp.int32), jnp.int32) > 0 for i in range(6)]

    def add(f, r, t, keep, values):
        rows = slice(FACE_ROWS * f + 8 * r, FACE_ROWS * f + 8 * r + 8)
        inc[t, rows] = jnp.where(keep, values, inc[t, rows])

    for j in range(2):
        part = rx[8 * j : 8 * j + 8]
        add(0, 2 * j, 0, low & has[0], part)
        add(0, 2 * j + 1, 0, low & has[0], roll(part, 64))
        part = rx[16 + 8 * j : 24 + 8 * j]
        add(1, 2 * j, 1, (lane >= 64) & has[1], roll(part, 64))
        add(1, 2 * j + 1, 1, (lane >= 64) & has[1], part)
    for r in range(4):
        for t in range(2):
            q = 2 * r + t
            add(2, r, t, (y == 0) & has[2], roll(rx[32:40], -8 * q))
            add(3, r, t, (y == 7) & has[3], roll(rx[40:48], 56 - 8 * q))
            add(4, r, t, (z == 0) & has[4], roll(rx[48:56], -q))
            add(5, r, t, (z == 7) & has[5], roll(rx[56:64], 7 - q))


def kernel(
    source_hbm, stiffness_hbm, relax_hbm, owners_hbm, material_hbm,
    landed, inc,
    src, stiff, relax, owner, mat, kpad, rpad, packer, moved, tx, rx,
    in_sem, halo_send, halo_recv, move_send, move_recv, side_sem, ready_sem, first_sem, relay, relay_send, relay_recv, nodes, picked,
):
    gx, gy, gz = (lax.axis_index(axis) for axis in ("gx", "gy", "gz"))
    loads = [
        *(
            pltpu.make_async_copy(stiffness_hbm.at[pl.ds(at, rows)], stiff.at[pl.ds(at, rows)], in_sem.at[6 + k])
            for k, (at, rows) in enumerate(((0, 32), (32, 32), (64, 32), (96, 29)))
        ),
        pltpu.make_async_copy(relax_hbm, relax, in_sem.at[1]),
        pltpu.make_async_copy(source_hbm.at[:, 0, pl.ds(0, LANES)], src.at[0, pl.ds(0, NODES)], in_sem.at[2]),
        pltpu.make_async_copy(source_hbm.at[:, 0, pl.ds(LANES, LANES)], src.at[1, pl.ds(0, NODES)], in_sem.at[5]),
        pltpu.make_async_copy(owners_hbm, owner, in_sem.at[3]),
        pltpu.make_async_copy(material_hbm, mat, in_sem.at[4]),
    ]
    for t in range(2):
        src[t, 120:128] = jnp.zeros((8, LANES), F32)
    for load in loads:
        load.start()
    rx[...] = jnp.zeros_like(rx)
    picked[...] = jnp.zeros_like(picked)

    my_y, my_x, my_c = gx // 16, (gx // 2) % 8, gx % 2

    def number(flag):
        return flag.astype(jnp.int32)

    def peer_at(chunk):
        dx, dy, dc = DX[chunk // 4], 1 - chunk // 2 % 2, 1 - chunk % 2
        return (my_y + dy) % 2, (my_x + dx) % 8, (my_c + dc) % 2

    def peer(chunk):
        y, x, c = peer_at(chunk)
        return y * 16 + x * 2 + c

    def rank_of(y, x, c):
        return jnp.maximum(2 * jnp.minimum(x, 8 - x) - 1 + number(x > 4), 0) * 4 + y * 2 + 1 - c

    def rank_at(index):
        return rank_of(index // 16, (index // 2) % 8, index % 2)

    line0 = (gy == 0) & (gz == 0)
    last = line0 & (gx == 0)
    rank = rank_of(my_y, my_x, my_c)
    my_rank = rank + 32 * number(last)

    def is_later(chunk):
        y, x, c = peer_at(chunk)
        return rank_of(y, x, c) + 32 * number(line0 & (y + x + c == 0)) > my_rank

    earlier_peers = jnp.where(last, 31, rank - number(line0 & (rank > 1)))
    later_peers = jnp.where(last, 0, 31 - number(line0) - earlier_peers)

    sides = (
        (gx + 1, gy, gz), (gx - 1, gy, gz), (gx, gy + 1, gz), (gx, gy - 1, gz), (gx, gy, gz + 1), (gx, gy, gz - 1),
    )
    there = (gx < 31, gx > 0, gy < 3, gy > 0, gz < 7, gz > 0)
    no = gx < 0
    to_last = (
        no, (gx == 1) & line0, no, (gx == 0) & (gy == 1) & (gz == 0), no, (gx == 0) & (gy == 0) & (gz == 1),
    )
    slow = last | to_last[1] | to_last[3] | to_last[5]
    usual = (rank_at(gx + 1) > rank, rank_at(gx - 1) > rank, gy < 2, gy == 3, gz >= 0, no)
    later = [there[i] & (to_last[i] | (jnp.logical_not(last) & usual[i])) for i in range(6)]
    earlier = [there[i] & jnp.logical_not(later[i]) for i in range(6)]
    greeted = earlier_peers + sum(number(earlier[i]) for i in range(2, 6)) + number(to_last[3] | to_last[5])

    def signal(semaphore, device):
        pl.semaphore_signal(semaphore, 1, device_id=device, device_id_type=MESH)

    barrier = pltpu.get_barrier_semaphore()
    for i in range(2, 6):
        pl.when(later[i])(functools.partial(signal, barrier, sides[i]))

    @pl.when(to_last[1])
    def _():
        signal(barrier, (0, 1, 0))
        signal(barrier, (0, 0, 1))

    @pl.when(jnp.logical_not(last))
    def _():
        for chunk in ORDER:
            pl.when(is_later(chunk))(functools.partial(signal, barrier, (peer(chunk), gy, gz)))

    def answer_sides():
        @pl.when(greeted > 0)
        def _():
            pl.semaphore_wait(barrier, greeted)

        for i in range(6):
            pl.when(earlier[i])(functools.partial(signal, side_sem.at[i ^ 1], sides[i]))

    @pl.when(last)
    def _():
        answer_sides()
        for chunk in ORDER:
            signal(first_sem, (peer(chunk), gy, gz))

    kpad[...] = jnp.zeros((LANES, LANES), F32)
    rpad[...] = jnp.zeros((8, LANES), F32)
    for load in loads[:5]:
        load.wait()
    kpad[0:NODES, 0:NODES] = stiff[...]
    rpad[0:1, 0:NODES] = relax[...]
    eye = iota((LANES, LANES), 0) == iota((LANES, LANES), 1)
    row = jnp.broadcast_to(rpad[0:1], (LANES, LANES))
    diag = jnp.where(eye, row, 0.0)
    col = jnp.sum(diag, axis=1, keepdims=True)
    scaled = col * kpad[...]
    step = jnp.where(eye, 1.0, 0.0) - scaled
    sum2 = 2.0 * diag - scaled * row
    step2 = full(step, step)
    sum4 = sum2 + full(step2, sum2)
    step4 = full(step2, step2)
    sum8 = sum4 + full(step4, sum4)
    elastic_op, acoustic_op = sum8 * (1.0 / 3.0), sum2

    for load in loads[5:]:
        load.wait()
    elastic = jnp.broadcast_to(mat[...], (LANES, COUNT)) > 0
    source = jnp.concatenate([src[0], src[1]], axis=1)
    field = full(jnp.concatenate([elastic_op, acoustic_op], axis=0), source)
    field = jnp.where(elastic, field[0:LANES], field[LANES : 2 * LANES])
    pick = face_rows()
    for t in range(2):
        nodes[t, 0:LANES] = field[:, LANES * t : LANES * (t + 1)]
        for f, (first, stride) in ((0, (0, 1)), (1, (100, 1)), (4, (0, 5)), (5, (4, 5))):
            picked[t, FACE_ROWS * f : FACE_ROWS * f + FACE] = nodes[t, pl.ds(first, FACE, stride=stride)]
        for f, first in ((2, 0), (3, 20)):
            for a in range(5):
                at = FACE_ROWS * f + 5 * a
                picked[t, at : at + 5] = nodes[t, 25 * a + first : 25 * a + first + 5]
    faces = jnp.concatenate([picked[0], picked[1]], axis=1)
    out = 2.0 * faces
    pack_halo(out, tx.at[0])

    def halo_copy(step, i):
        at, rows = HALO[i]
        return pltpu.make_async_remote_copy(
            src_ref=tx.at[step, pl.ds(at, rows)],
            dst_ref=rx.at[step, pl.ds(at, rows)],
            send_sem=halo_send.at[i],
            recv_sem=halo_recv.at[step, i],
            device_id=sides[i],
            device_id_type=MESH,
        )

    def halo_start(step, i, when):
        @pl.when(when)
        def _():
            halo_copy(step, i).start()

    def halo_wait_recv(step):
        for i in range(6):
            @pl.when(there[i ^ 1])
            def _():
                halo_copy(step, i).wait_recv()

    def halo_wait_send(step):
        for i in range(6):
            @pl.when(there[i])
            def _():
                halo_copy(step, i).wait_send()

    pl.when(jnp.logical_not(last))(answer_sides)

    for i in (2, 3, 4, 5, 0, 1):
        halo_start(0, i, earlier[i])

    @pl.when(jnp.logical_not(last))
    def _():
        for chunk in ORDER:
            pl.when(jnp.logical_not(is_later(chunk)))(
                functools.partial(signal, ready_sem, (peer(chunk), gy, gz))
            )

    def relay_in(i, k):
        at, rows = HALO[i]
        return pltpu.make_async_remote_copy(
            src_ref=tx.at[0, pl.ds(at, rows)],
            dst_ref=relay.at[pl.ds(8 * k, rows)],
            send_sem=halo_send.at[i],
            recv_sem=relay_recv.at[k],
            device_id=(1, 0, 0),
            device_id_type=MESH,
        )

    def relay_out(i, k):
        at, rows = HALO[i]
        return pltpu.make_async_remote_copy(
            src_ref=relay.at[pl.ds(8 * k, rows)],
            dst_ref=rx.at[0, pl.ds(at, rows)],
            send_sem=relay_send.at[k],
            recv_sem=halo_recv.at[0, i],
            device_id=(0, 0, 0),
            device_id_type=MESH,
        )

    for k, i in enumerate((3, 5)):
        pl.when(to_last[i])(lambda k=k, i=i: relay_in(i, k).start())

    def halo_start_later():
        for i in range(6):
            @pl.when(later[i] & jnp.logical_not(to_last[i]))
            def _():
                pl.semaphore_wait(side_sem.at[i], 1)
                halo_copy(0, i).start()

    halo_start_later()

    shift_inside(out, inc)
    ops = []
    for op in (elastic_op, acoustic_op):
        high, low = halves(op)
        nodes = matmul_t(high, pick) + matmul_t(low, pick)
        high, low = halves(nodes)
        ops.append((high, low))
    on_nodes = [jnp.concatenate([ops[0][i], ops[1][i]], axis=0) for i in range(2)]
    on_faces = [
        jnp.concatenate([matmul(pick, ops[0][i]), matmul(pick, ops[1][i])], axis=0).astype(BF16) for i in range(2)
    ]

    names = owner[...]
    named = iota((GROUPS, COUNT), 0) == jnp.broadcast_to(names, (GROUPS, COUNT))
    before = jnp.where(iota((COUNT, COUNT), 0) < iota((COUNT, COUNT), 1), 1.0, 0.0).astype(BF16)
    counts = matmul(jnp.where(named, 1.0, 0.0).astype(BF16), before)
    place = jnp.sum(jnp.where(named, counts, 0.0), axis=0, keepdims=True).astype(jnp.int32)
    ahead = ((names >> 1) - my_x) & 7
    near = jnp.minimum(ahead, 8 - ahead)
    ring = jnp.maximum(7 - 2 * near + jnp.where(ahead > 4, 1, 0), 0)
    chunk = 4 * ring + 2 * (1 - ((names >> 4) ^ my_y)) + 1 - ((names & 1) ^ my_c)
    slot = chunk * CAP + place
    for k in range(4):
        here = iota((LANES, COUNT), 0) + k * LANES == jnp.broadcast_to(slot, (LANES, COUNT))
        packer[k * LANES : (k + 1) * LANES] = jnp.where(here, 1.0, 0.0).astype(BF16)

    @pl.when(to_last[1])
    def _():
        pl.semaphore_wait(side_sem.at[1], 1)
        halo_copy(0, 1).start()
        for k, i in enumerate((3, 5)):
            relay_in(i, k).wait_recv()
            relay_out(i, k).start()

    halo_wait_recv(0)
    add_halo(rx.at[0], inc, there)

    incoming = jnp.concatenate([inc[0], inc[1]], axis=1)
    high, low = halves(incoming)

    def on_traces(op):
        return matmul(op[0], high) + matmul(op[0], low) + matmul(op[1], high)

    change = on_traces(on_nodes)
    field = field + jnp.where(elastic, change[0:LANES], change[LANES : 2 * LANES])
    both = jnp.concatenate(halves(field), axis=0)
    mine = pl.ds(pl.multiple_of(gx * CAP, CAP), CAP)

    def move(chunk, device=None):
        return pltpu.make_async_remote_copy(
            src_ref=moved.at[pl.ds(pl.multiple_of(chunk * CAP, CAP), CAP)],
            dst_ref=landed.at[mine],
            send_sem=move_send.at[0],
            recv_sem=move_recv.at[0],
            device_id=device or (peer(chunk), gy, gz),
            device_id_type=MESH,
        )

    @pl.when(later_peers > 0)
    def _():
        pl.semaphore_wait(ready_sem, later_peers)

    for k in range(4):
        part = matmul_t(packer[k * LANES : (k + 1) * LANES], both)
        moved[k * LANES : (k + 1) * LANES] = part[:, 0:LANES] + part[:, LANES : 2 * LANES]
        for chunk in ORDER[8 * k : 8 * k + 8]:
            held = line0 & (peer(chunk) == 0)
            held = held if chunk // 4 == 1 else held | slow
            pl.when(jnp.logical_not(held))(lambda chunk=chunk: move(chunk).start())
    landed[mine] = moved[SLOTS - CAP : SLOTS]

    change = on_traces(on_faces)
    face_elastic = jnp.broadcast_to(mat[...], (STACK, COUNT)) > 0
    faces = faces + jnp.where(face_elastic, change[0:STACK], change[STACK : 2 * STACK])
    out = 2.0 * faces - incoming
    pack_halo(out, tx.at[1])
    for i in (3, 5):
        @pl.when(to_last[i])
        def _():
            pl.semaphore_wait(side_sem.at[i], 1)
    halo_wait_send(0)
    for i in range(6):
        halo_start(1, i, there[i])

    @pl.when(slow)
    def _():
        for chunk in LATE_ORDER:
            pl.when(jnp.logical_not(line0 & (peer(chunk) == 0)))(lambda chunk=chunk: move(chunk).start())

    @pl.when(line0 & (gx > 0))
    def _():
        pl.semaphore_wait(first_sem, 1)
        ahead = (8 - my_x) % 8
        ring = jnp.maximum(7 - 2 * jnp.minimum(ahead, 8 - ahead) + number(ahead > 4), 0)
        move(4 * ring + 2 * (1 - my_y) + 1 - my_c, (0, gy, gz)).start()

    shift_inside(out, inc)
    halo_wait_recv(1)
    add_halo(rx.at[1], inc, there)
    chunks = landed.at[pl.ds(0, SLOTS - CAP)]
    pltpu.make_async_copy(chunks, chunks, move_recv.at[0]).wait()
    halo_wait_send(1)

    @pl.when(to_last[1])
    def _():
        for k, i in enumerate((3, 5)):
            relay_out(i, k).wait_send()

    chunks = moved.at[pl.ds(0, SLOTS - CAP)]
    pltpu.make_async_copy(chunks, chunks, move_send.at[0]).wait()


def finish(landed, inc, settled_hbm, incoming_hbm, turned, out_sem):
    results = []
    for k in range(4):
        turned[k] = landed[k * LANES : (k + 1) * LANES].T
        results.append(
            pltpu.make_async_copy(
                turned.at[k, pl.ds(0, NODES)], settled_hbm.at[:, 0, pl.ds(k * LANES, LANES)], out_sem.at[2 + k]
            )
        )
        results[-1].start()
    for t in range(2):
        results.append(
            pltpu.make_async_copy(
                inc.at[t, :, pl.ds(0, FACE)], incoming_hbm.at[:, :, 0, pl.ds(t * LANES, LANES)], out_sem.at[t]
            )
        )
        results[-1].start()
    for copy in results:
        copy.wait()


def shards(source, stiffness, relax, owners, material):
    anywhere = pl.BlockSpec(memory_space=pl.ANY)
    vmem = pl.BlockSpec(memory_space=pltpu.VMEM)
    operands = (
        source.reshape(NODES, 1, COUNT),
        stiffness,
        relax.reshape(1, NODES),
        owners.reshape(1, COUNT),
        material.reshape(1, COUNT),
    )
    landed, inc = pl.pallas_call(
        kernel,
        out_shape=(pltpu.VMEM((SLOTS, LANES), F32), pltpu.VMEM((2, STACK, LANES), F32)),
        in_specs=[anywhere] * 5,
        out_specs=(vmem, vmem),
        scratch_shapes=[
            pltpu.VMEM((2, LANES, LANES), F32),
            pltpu.VMEM((NODES, NODES), F32),
            pltpu.VMEM((1, NODES), F32),
            pltpu.VMEM((1, COUNT), jnp.int32),
            pltpu.VMEM((1, COUNT), jnp.int32),
            pltpu.VMEM((LANES, LANES), F32),
            pltpu.VMEM((8, LANES), F32),
            pltpu.VMEM((SLOTS, COUNT), BF16),
            pltpu.VMEM((SLOTS, LANES), F32),
            pltpu.VMEM((2, HALO_ROWS, LANES), F32),
            pltpu.VMEM((2, HALO_ROWS, LANES), F32),
            pltpu.SemaphoreType.DMA((10,)),
            pltpu.SemaphoreType.DMA((6,)),
            pltpu.SemaphoreType.DMA((2, 6)),
            pltpu.SemaphoreType.DMA((1,)),
            pltpu.SemaphoreType.DMA((1,)),
            pltpu.SemaphoreType.REGULAR((6,)),
            pltpu.SemaphoreType.REGULAR,
            pltpu.SemaphoreType.REGULAR,
            pltpu.VMEM((16, LANES), F32),
            pltpu.SemaphoreType.DMA((2,)),
            pltpu.SemaphoreType.DMA((2,)),
            pltpu.VMEM((2, LANES + 8, LANES), F32),
            pltpu.VMEM((2, STACK, LANES), F32),
        ],
        compiler_params=pltpu.CompilerParams(
            collective_id=0, has_side_effects=True, vmem_limit_bytes=32 * 1024 * 1024
        ),
    )(*(pltpu.with_memory_space_constraint(x, pltpu.HBM) for x in operands))
    settled, incoming = pl.pallas_call(
        finish,
        out_shape=(pltpu.HBM((NODES, 1, SLOTS), F32), pltpu.HBM((6, FACE, 1, COUNT), F32)),
        in_specs=(vmem, vmem),
        out_specs=(anywhere, anywhere),
        scratch_shapes=[pltpu.VMEM((4, LANES, LANES), F32), pltpu.SemaphoreType.DMA((6,))],
        compiler_params=pltpu.CompilerParams(vmem_limit_bytes=32 * 1024 * 1024),
    )(landed, inc.reshape(2, 6, FACE_ROWS, LANES))
    return (
        settled.reshape(1, 1, 1, NODES, SLOTS),
        incoming.reshape(1, 1, 1, 6, FACE, COUNT),
    )


def solution(mesh):
    return jax.shard_map(
        shards,
        mesh=mesh,
        in_specs=(
            P("gx", "gy", "gz", None, None),
            P(),
            P(),
            P("gx", "gy", "gz", None, None),
            P("gx", "gy", "gz", None),
        ),
        out_specs=(P("gx", "gy", "gz", None, None), P("gx", "gy", "gz", None, None, None)),
        check_vma=False,
    )
```

```python
import functools

import jax
import jax.numpy as jnp
from jax import lax
from jax.experimental import pallas as pl
from jax.experimental.pallas import tpu as pltpu
from jax.sharding import PartitionSpec as P

NODES = 125
FACE = 25
LANES = 128
COUNT = 256
SLOTS = 512
CAP = 16
GROUPS = 32
FACE_ROWS = 32
STACK = 6 * FACE_ROWS
MESH = pl.DeviceIdType.MESH
F32 = jnp.float32
BF16 = jnp.bfloat16
HIGHEST = lax.Precision.HIGHEST

HALO = ((0, 16), (16, 16), (32, 8), (40, 8), (48, 8), (56, 8))
HALO_ROWS = 64
DX = (4, 3, 5, 2, 6, 1, 7, 0)
ORDER = range(GROUPS - 1)
LATE_ORDER = (20, 24, 21, 25, 22, 26, 23, 27, 30, 12, 16, 13, 17, 14, 18, 15, 19, 0, 8, 1, 9, 2, 10, 3, 11, 28, 29)


def iota(shape, dim):
    return lax.broadcasted_iota(jnp.int32, shape, dim)


def matmul(left, right):
    return lax.dot_general(
        left, right, (((1,), (0,)), ((), ())), preferred_element_type=F32
    )


def matmul_t(left, right):
    return lax.dot_general(
        left, right, (((1,), (1,)), ((), ())), preferred_element_type=F32
    )


def full(left, right):
    return lax.dot_general(
        left, right, (((1,), (0,)), ((), ())), precision=lax.Precision.HIGH, preferred_element_type=F32
    )


def halves(values):
    high = values.astype(BF16)
    return high, (values - high.astype(F32)).astype(BF16)


def roll(values, shift):
    shift = shift % LANES
    return pltpu.roll(values, shift, 1) if shift else values


def face_rows():
    m = iota((FACE_ROWS, LANES), 0)
    node = iota((FACE_ROWS, LANES), 1)
    a = sum((m >= cut).astype(jnp.int32) for cut in (5, 10, 15, 20))
    b = m - 5 * a
    picks = (m, m + 100, 25 * a + b, 25 * a + b + 20, 5 * m, 5 * m + 4)
    faces = [jnp.where((node == pick) & (m < FACE), 1.0, 0.0) for pick in picks]
    return jnp.concatenate(faces, axis=0).astype(BF16)


def pieces(face):
    return [(r, t, face[8 * r : 8 * r + 8, LANES * t : LANES * t + LANES]) for r in range(4) for t in range(2)]


def total(terms):
    while len(terms) > 1:
        terms = [sum(terms[i : i + 2]) for i in range(0, len(terms), 2)]
    return terms[0]


def pack_halo(out, tx):
    lane = iota((8, LANES), 1)
    z, y = lane & 7, (lane >> 3) & 7
    low = lane < 64
    face = lambda f: out[FACE_ROWS * f : FACE_ROWS * (f + 1)]
    piece = {f: {(r, t): v for r, t, v in pieces(face(f))} for f in range(6)}
    for j in range(2):
        tx[8 * j : 8 * j + 8] = jnp.where(low, roll(piece[1][2 * j, 1], 64), piece[1][2 * j + 1, 1])
        tx[16 + 8 * j : 24 + 8 * j] = jnp.where(low, piece[0][2 * j, 0], roll(piece[0][2 * j + 1, 0], 64))

    def gather(f, keep, shift):
        return total([
            roll(jnp.where(keep, piece[f][r, t], 0.0), shift(2 * r + t)) for r in range(4) for t in range(2)
        ])

    tx[32:40] = gather(3, y == 7, lambda q: 8 * q - 56)
    tx[40:48] = gather(2, y == 0, lambda q: 8 * q)
    tx[48:56] = gather(5, z == 7, lambda q: q - 7)
    tx[56:64] = gather(4, z == 0, lambda q: q)


def shift_inside(out, inc):
    lane = iota((FACE_ROWS, LANES), 1)
    z, y = lane & 7, (lane >> 3) & 7
    low = lane < 64
    tile = lambda f, t: out[FACE_ROWS * f : FACE_ROWS * (f + 1), LANES * t : LANES * (t + 1)]

    def put(f, t, values):
        inc[t, FACE_ROWS * f : FACE_ROWS * (f + 1)] = values

    a, b = roll(tile(1, 0), 64), roll(tile(1, 1), 64)
    put(0, 0, jnp.where(low, 0.0, a))
    put(0, 1, jnp.where(low, a, b))
    a, b = roll(tile(0, 0), 64), roll(tile(0, 1), 64)
    put(1, 0, jnp.where(low, a, b))
    put(1, 1, jnp.where(low, b, 0.0))
    for t in range(2):
        put(2, t, jnp.where(y == 0, 0.0, roll(tile(3, t), 8)))
        put(3, t, jnp.where(y == 7, 0.0, roll(tile(2, t), -8)))
        put(4, t, jnp.where(z == 0, 0.0, roll(tile(5, t), 1)))
        put(5, t, jnp.where(z == 7, 0.0, roll(tile(4, t), -1)))


def add_halo(rx, inc, inner):
    lane = iota((8, LANES), 1)
    z, y = lane & 7, (lane >> 3) & 7
    low = lane < 64
    has = [jnp.full((8, LANES), inner[i ^ 1].astype(jnp.int32), jnp.int32) > 0 for i in range(6)]

    def add(f, r, t, keep, values):
        rows = slice(FACE_ROWS * f + 8 * r, FACE_ROWS * f + 8 * r + 8)
        inc[t, rows] = jnp.where(keep, values, inc[t, rows])

    for j in range(2):
        part = rx[8 * j : 8 * j + 8]
        add(0, 2 * j, 0, low & has[0], part)
        add(0, 2 * j + 1, 0, low & has[0], roll(part, 64))
        part = rx[16 + 8 * j : 24 + 8 * j]
        add(1, 2 * j, 1, (lane >= 64) & has[1], roll(part, 64))
        add(1, 2 * j + 1, 1, (lane >= 64) & has[1], part)
    for r in range(4):
        for t in range(2):
            q = 2 * r + t
            add(2, r, t, (y == 0) & has[2], roll(rx[32:40], -8 * q))
            add(3, r, t, (y == 7) & has[3], roll(rx[40:48], 56 - 8 * q))
            add(4, r, t, (z == 0) & has[4], roll(rx[48:56], -q))
            add(5, r, t, (z == 7) & has[5], roll(rx[56:64], 7 - q))


def kernel(
    source_hbm, stiffness_hbm, relax_hbm, owners_hbm, material_hbm,
    landed, inc,
    src, stiff, relax, owner, mat, kpad, rpad, packer, moved, tx, rx,
    in_sem, halo_send, halo_recv, move_send, move_recv, side_sem, ready_sem, first_sem, relay, nodes, picked,
):
    gx, gy, gz = (lax.axis_index(axis) for axis in ("gx", "gy", "gz"))
    loads = [
        *(
            pltpu.make_async_copy(stiffness_hbm.at[pl.ds(at, rows)], stiff.at[pl.ds(at, rows)], in_sem.at[5 + k])
            for k, (at, rows) in enumerate(((0, 32), (32, 32), (64, 32), (96, 29)))
        ),
        pltpu.make_async_copy(relax_hbm, relax, in_sem.at[1]),
        pltpu.make_async_copy(source_hbm.at[:, 0, pl.ds(0, LANES)], src.at[0, pl.ds(0, NODES)], in_sem.at[2]),
        pltpu.make_async_copy(source_hbm.at[:, 0, pl.ds(LANES, LANES)], src.at[1, pl.ds(0, NODES)], in_sem.at[0]),
        pltpu.make_async_copy(owners_hbm, owner, in_sem.at[3]),
        pltpu.make_async_copy(material_hbm, mat, in_sem.at[4]),
    ]
    for t in range(2):
        src[t, 120:128] = jnp.zeros((8, LANES), F32)
    for load in loads:
        load.start()
    rx[...] = jnp.zeros_like(rx)
    picked[...] = jnp.zeros_like(picked)

    my_y, my_x, my_c = gx // 16, (gx // 2) % 8, gx % 2

    def number(flag):
        return flag.astype(jnp.int32)

    def peer_at(chunk):
        dx, dy, dc = DX[chunk // 4], 1 - chunk // 2 % 2, 1 - chunk % 2
        return (my_y + dy) % 2, (my_x + dx) % 8, (my_c + dc) % 2

    def peer(chunk):
        y, x, c = peer_at(chunk)
        return y * 16 + x * 2 + c

    def rank_of(y, x, c):
        return jnp.maximum(2 * jnp.minimum(x, 8 - x) - 1 + number(x > 4), 0) * 4 + y * 2 + 1 - c

    def rank_at(index):
        return rank_of(index // 16, (index // 2) % 8, index % 2)

    line0 = (gy == 0) & (gz == 0)
    last = line0 & (gx == 0)
    rank = rank_of(my_y, my_x, my_c)
    my_rank = rank + 32 * number(last)

    def is_later(chunk):
        y, x, c = peer_at(chunk)
        return rank_of(y, x, c) + 32 * number(line0 & (y + x + c == 0)) > my_rank

    earlier_peers = jnp.where(last, 31, rank - number(line0 & (rank > 1)))
    later_peers = jnp.where(last, 0, 31 - number(line0) - earlier_peers)

    sides = (
        (gx + 1, gy, gz), (gx - 1, gy, gz), (gx, gy + 1, gz), (gx, gy - 1, gz), (gx, gy, gz + 1), (gx, gy, gz - 1),
    )
    there = (gx < 31, gx > 0, gy < 3, gy > 0, gz < 7, gz > 0)
    no = gx < 0
    to_last = (
        no, (gx == 1) & line0, no, (gx == 0) & (gy == 1) & (gz == 0), no, (gx == 0) & (gy == 0) & (gz == 1),
    )
    slow = last | to_last[1] | to_last[3] | to_last[5]
    usual = (rank_at(gx + 1) > rank, rank_at(gx - 1) > rank, gy < 2, gy == 3, gz >= 0, no)
    later = [there[i] & (to_last[i] | (jnp.logical_not(last) & usual[i])) for i in range(6)]
    earlier = [there[i] & jnp.logical_not(later[i]) for i in range(6)]
    greeted = earlier_peers + sum(number(earlier[i]) for i in range(2, 6)) + number(to_last[3] | to_last[5])

    def signal(semaphore, device):
        pl.semaphore_signal(semaphore, 1, device_id=device, device_id_type=MESH)

    barrier = pltpu.get_barrier_semaphore()
    for i in range(2, 6):
        pl.when(later[i])(functools.partial(signal, barrier, sides[i]))

    @pl.when(to_last[1])
    def _():
        signal(barrier, (0, 1, 0))
        signal(barrier, (0, 0, 1))

    @pl.when(jnp.logical_not(last))
    def _():
        for chunk in ORDER:
            pl.when(is_later(chunk))(functools.partial(signal, barrier, (peer(chunk), gy, gz)))

    def answer_sides():
        @pl.when(greeted > 0)
        def _():
            pl.semaphore_wait(barrier, greeted)

        for i in range(6):
            pl.when(earlier[i])(functools.partial(signal, side_sem.at[i ^ 1], sides[i]))

    @pl.when(last)
    def _():
        answer_sides()
        for chunk in ORDER:
            signal(first_sem, (peer(chunk), gy, gz))

    kpad[...] = jnp.zeros((LANES, LANES), F32)
    rpad[...] = jnp.zeros((8, LANES), F32)
    for load in loads[:5]:
        load.wait()
    kpad[0:NODES, 0:NODES] = stiff[...]
    rpad[0:1, 0:NODES] = relax[...]
    eye = iota((LANES, LANES), 0) == iota((LANES, LANES), 1)
    row = jnp.broadcast_to(rpad[0:1], (LANES, LANES))
    diag = jnp.where(eye, row, 0.0)
    col = jnp.sum(diag, axis=1, keepdims=True)
    scaled = col * kpad[...]
    step = jnp.where(eye, 1.0, 0.0) - scaled
    sum2 = 2.0 * diag - scaled * row
    step2 = full(step, step)
    sum4 = sum2 + full(step2, sum2)
    step4 = full(step2, step2)
    sum8 = sum4 + full(step4, sum4)
    elastic_op, acoustic_op = sum8 * (1.0 / 3.0), sum2

    for load in loads[5:]:
        load.wait()
    elastic = jnp.broadcast_to(mat[...], (LANES, COUNT)) > 0
    source = jnp.concatenate([src[0], src[1]], axis=1)
    field = full(jnp.concatenate([elastic_op, acoustic_op], axis=0), source)
    field = jnp.where(elastic, field[0:LANES], field[LANES : 2 * LANES])
    pick = face_rows()
    for t in range(2):
        nodes[t, 0:LANES] = field[:, LANES * t : LANES * (t + 1)]
        for f, (first, stride) in ((0, (0, 1)), (1, (100, 1)), (4, (0, 5)), (5, (4, 5))):
            picked[t, FACE_ROWS * f : FACE_ROWS * f + FACE] = nodes[t, pl.ds(first, FACE, stride=stride)]
        for f, first in ((2, 0), (3, 20)):
            for a in range(5):
                at = FACE_ROWS * f + 5 * a
                picked[t, at : at + 5] = nodes[t, 25 * a + first : 25 * a + first + 5]
    faces = jnp.concatenate([picked[0], picked[1]], axis=1)
    out = 2.0 * faces
    pack_halo(out, tx.at[0])

    def halo_copy(step, i):
        at, rows = HALO[i]
        return pltpu.make_async_remote_copy(
            src_ref=tx.at[step, pl.ds(at, rows)],
            dst_ref=rx.at[step, pl.ds(at, rows)],
            send_sem=halo_send.at[i],
            recv_sem=halo_recv.at[step, i],
            device_id=sides[i],
            device_id_type=MESH,
        )

    def halo_start(step, i, when):
        @pl.when(when)
        def _():
            halo_copy(step, i).start()

    def halo_wait_recv(step):
        for i in range(6):
            @pl.when(there[i ^ 1])
            def _():
                halo_copy(step, i).wait_recv()

    def halo_wait_send(step):
        for i in range(6):
            @pl.when(there[i])
            def _():
                halo_copy(step, i).wait_send()

    pl.when(jnp.logical_not(last))(answer_sides)

    for i in (2, 3, 4, 5, 0, 1):
        halo_start(0, i, earlier[i])

    @pl.when(jnp.logical_not(last))
    def _():
        for chunk in ORDER:
            pl.when(jnp.logical_not(is_later(chunk)))(
                functools.partial(signal, ready_sem, (peer(chunk), gy, gz))
            )

    def relay_in(i, k):
        at, rows = HALO[i]
        return pltpu.make_async_remote_copy(
            src_ref=tx.at[0, pl.ds(at, rows)],
            dst_ref=relay.at[pl.ds(8 * k, rows)],
            send_sem=halo_send.at[i],
            recv_sem=halo_recv.at[0, i - 1],
            device_id=(1, 0, 0),
            device_id_type=MESH,
        )

    def relay_out(i, k):
        at, rows = HALO[i]
        return pltpu.make_async_remote_copy(
            src_ref=relay.at[pl.ds(8 * k, rows)],
            dst_ref=rx.at[0, pl.ds(at, rows)],
            send_sem=halo_send.at[i],
            recv_sem=halo_recv.at[0, i],
            device_id=(0, 0, 0),
            device_id_type=MESH,
        )

    for k, i in enumerate((3, 5)):
        pl.when(to_last[i])(lambda k=k, i=i: relay_in(i, k).start())

    def halo_start_later():
        for i in range(6):
            @pl.when(later[i] & jnp.logical_not(to_last[i]))
            def _():
                pl.semaphore_wait(side_sem.at[i], 1)
                halo_copy(0, i).start()

    halo_start_later()

    shift_inside(out, inc)
    ops = []
    for op in (elastic_op, acoustic_op):
        high, low = halves(op)
        nodes = matmul_t(high, pick) + matmul_t(low, pick)
        high, low = halves(nodes)
        ops.append((high, low))
    on_nodes = [jnp.concatenate([ops[0][i], ops[1][i]], axis=0) for i in range(2)]
    on_faces = [
        jnp.concatenate([matmul(pick, ops[0][i]), matmul(pick, ops[1][i])], axis=0).astype(BF16) for i in range(2)
    ]

    names = owner[...]
    named = iota((GROUPS, COUNT), 0) == jnp.broadcast_to(names, (GROUPS, COUNT))
    before = jnp.where(iota((COUNT, COUNT), 0) < iota((COUNT, COUNT), 1), 1.0, 0.0).astype(BF16)
    counts = matmul(jnp.where(named, 1.0, 0.0).astype(BF16), before)
    place = jnp.sum(jnp.where(named, counts, 0.0), axis=0, keepdims=True).astype(jnp.int32)
    ahead = ((names >> 1) - my_x) & 7
    near = jnp.minimum(ahead, 8 - ahead)
    ring = jnp.maximum(7 - 2 * near + jnp.where(ahead > 4, 1, 0), 0)
    chunk = 4 * ring + 2 * (1 - ((names >> 4) ^ my_y)) + 1 - ((names & 1) ^ my_c)
    slot = chunk * CAP + place
    for k in range(4):
        here = iota((LANES, COUNT), 0) + k * LANES == jnp.broadcast_to(slot, (LANES, COUNT))
        packer[k * LANES : (k + 1) * LANES] = jnp.where(here, 1.0, 0.0).astype(BF16)

    @pl.when(to_last[1])
    def _():
        pl.semaphore_wait(side_sem.at[1], 1)
        halo_copy(0, 1).start()
        for k, i in enumerate((3, 5)):
            relay_in(i, k).wait_recv()
            relay_out(i, k).start()

    halo_wait_recv(0)
    add_halo(rx.at[0], inc, there)

    incoming = jnp.concatenate([inc[0], inc[1]], axis=1)
    high, low = halves(incoming)

    def on_traces(op):
        return matmul(op[0], high) + matmul(op[0], low) + matmul(op[1], high)

    change = on_traces(on_nodes)
    field = field + jnp.where(elastic, change[0:LANES], change[LANES : 2 * LANES])
    both = jnp.concatenate(halves(field), axis=0)
    mine = pl.ds(pl.multiple_of(gx * CAP, CAP), CAP)

    def move(chunk, device=None):
        return pltpu.make_async_remote_copy(
            src_ref=moved.at[pl.ds(pl.multiple_of(chunk * CAP, CAP), CAP)],
            dst_ref=landed.at[mine],
            send_sem=move_send.at[0],
            recv_sem=move_recv.at[0],
            device_id=device or (peer(chunk), gy, gz),
            device_id_type=MESH,
        )

    @pl.when(later_peers > 0)
    def _():
        pl.semaphore_wait(ready_sem, later_peers)

    for k in range(4):
        part = matmul_t(packer[k * LANES : (k + 1) * LANES], both)
        moved[k * LANES : (k + 1) * LANES] = part[:, 0:LANES] + part[:, LANES : 2 * LANES]
        for chunk in ORDER[8 * k : 8 * k + 8]:
            held = line0 & (peer(chunk) == 0)
            held = held if chunk // 4 == 1 else held | slow
            pl.when(jnp.logical_not(held))(lambda chunk=chunk: move(chunk).start())
    landed[mine] = moved[SLOTS - CAP : SLOTS]

    change = on_traces(on_faces)
    face_elastic = jnp.broadcast_to(mat[...], (STACK, COUNT)) > 0
    faces = faces + jnp.where(face_elastic, change[0:STACK], change[STACK : 2 * STACK])
    out = 2.0 * faces - incoming
    pack_halo(out, tx.at[1])
    for i in (3, 5):
        @pl.when(to_last[i])
        def _():
            pl.semaphore_wait(side_sem.at[i], 1)
    halo_wait_send(0)
    for i in range(6):
        halo_start(1, i, there[i])

    @pl.when(slow)
    def _():
        for chunk in LATE_ORDER:
            pl.when(jnp.logical_not(line0 & (peer(chunk) == 0)))(lambda chunk=chunk: move(chunk).start())

    @pl.when(line0 & (gx > 0))
    def _():
        pl.semaphore_wait(first_sem, 1)
        ahead = (8 - my_x) % 8
        ring = jnp.maximum(7 - 2 * jnp.minimum(ahead, 8 - ahead) + number(ahead > 4), 0)
        move(4 * ring + 2 * (1 - my_y) + 1 - my_c, (0, gy, gz)).start()

    shift_inside(out, inc)
    halo_wait_recv(1)
    add_halo(rx.at[1], inc, there)
    chunks = landed.at[pl.ds(0, SLOTS - CAP)]
    pltpu.make_async_copy(chunks, chunks, move_recv.at[0]).wait()
    halo_wait_send(1)

    @pl.when(to_last[1])
    def _():
        for k, i in enumerate((3, 5)):
            relay_out(i, k).wait_send()

    chunks = moved.at[pl.ds(0, SLOTS - CAP)]
    pltpu.make_async_copy(chunks, chunks, move_send.at[0]).wait()


def finish(landed, inc, settled_hbm, incoming_hbm, turned, out_sem):
    results = []
    for k in range(4):
        turned[k] = landed[k * LANES : (k + 1) * LANES].T
        results.append(
            pltpu.make_async_copy(
                turned.at[k, pl.ds(0, NODES)], settled_hbm.at[:, 0, pl.ds(k * LANES, LANES)], out_sem.at[2 + k]
            )
        )
        results[-1].start()
    for t in range(2):
        results.append(
            pltpu.make_async_copy(
                inc.at[t, :, pl.ds(0, FACE)], incoming_hbm.at[:, :, 0, pl.ds(t * LANES, LANES)], out_sem.at[t]
            )
        )
        results[-1].start()
    for copy in results:
        copy.wait()


def shards(source, stiffness, relax, owners, material):
    anywhere = pl.BlockSpec(memory_space=pl.ANY)
    vmem = pl.BlockSpec(memory_space=pltpu.VMEM)
    operands = (
        source.reshape(NODES, 1, COUNT),
        stiffness,
        relax.reshape(1, NODES),
        owners.reshape(1, COUNT),
        material.reshape(1, COUNT),
    )
    landed, inc = pl.pallas_call(
        kernel,
        out_shape=(pltpu.VMEM((SLOTS, LANES), F32), pltpu.VMEM((2, STACK, LANES), F32)),
        in_specs=[anywhere] * 5,
        out_specs=(vmem, vmem),
        scratch_shapes=[
            pltpu.VMEM((2, LANES, LANES), F32),
            pltpu.VMEM((NODES, NODES), F32),
            pltpu.VMEM((1, NODES), F32),
            pltpu.VMEM((1, COUNT), jnp.int32),
            pltpu.VMEM((1, COUNT), jnp.int32),
            pltpu.VMEM((LANES, LANES), F32),
            pltpu.VMEM((8, LANES), F32),
            pltpu.VMEM((SLOTS, COUNT), BF16),
            pltpu.VMEM((SLOTS, LANES), F32),
            pltpu.VMEM((2, HALO_ROWS, LANES), F32),
            pltpu.VMEM((2, HALO_ROWS, LANES), F32),
            pltpu.SemaphoreType.DMA((9,)),
            pltpu.SemaphoreType.DMA((6,)),
            pltpu.SemaphoreType.DMA((2, 6)),
            pltpu.SemaphoreType.DMA((1,)),
            pltpu.SemaphoreType.DMA((1,)),
            pltpu.SemaphoreType.REGULAR((6,)),
            pltpu.SemaphoreType.REGULAR,
            pltpu.SemaphoreType.REGULAR,
            pltpu.VMEM((16, LANES), F32),
            pltpu.VMEM((2, LANES + 8, LANES), F32),
            pltpu.VMEM((2, STACK, LANES), F32),
        ],
        compiler_params=pltpu.CompilerParams(
            collective_id=0, has_side_effects=True, vmem_limit_bytes=32 * 1024 * 1024
        ),
    )(*(pltpu.with_memory_space_constraint(x, pltpu.HBM) for x in operands))
    settled, incoming = pl.pallas_call(
        finish,
        out_shape=(pltpu.HBM((NODES, 1, SLOTS), F32), pltpu.HBM((6, FACE, 1, COUNT), F32)),
        in_specs=(vmem, vmem),
        out_specs=(anywhere, anywhere),
        scratch_shapes=[pltpu.VMEM((4, LANES, LANES), F32), pltpu.SemaphoreType.DMA((6,))],
        compiler_params=pltpu.CompilerParams(vmem_limit_bytes=32 * 1024 * 1024),
    )(landed, inc.reshape(2, 6, FACE_ROWS, LANES))
    return (
        settled.reshape(1, 1, 1, NODES, SLOTS),
        incoming.reshape(1, 1, 1, 6, FACE, COUNT),
    )


def solution(mesh):
    return jax.shard_map(
        shards,
        mesh=mesh,
        in_specs=(
            P("gx", "gy", "gz", None, None),
            P(),
            P(),
            P("gx", "gy", "gz", None, None),
            P("gx", "gy", "gz", None),
        ),
        out_specs=(P("gx", "gy", "gz", None, None), P("gx", "gy", "gz", None, None, None)),
        check_vma=False,
    )
```
